512 devices in a mesh: dp: 128 (over y, z_hi, x, core), tensor: 4 (over z_lo).
Axes of the slice: x: 4, y: 4, z: 16 (z_hi: 4, z_lo: 4; z = z_hi * 4 + z_lo), core: 2. Of those that a mesh axis runs over, the one named last changes fastest.
Arguments:
- teacher_rows: bfloat16 [16384, 16384], P('dp', 'tensor'), may hold values from -24 to 24
- row_map: int32 [16384], P('dp'), may hold values from 0 to 16383, as said below
- student_hidden: bfloat16 [16384, 8192], P('dp', 'tensor'), may hold values from -6 to 6
- projected: bfloat16 [16384, 8192], P('dp', 'tensor'), may hold values from -6 to 6
- mlp_input: bfloat16 [16384, 8192], P('dp', 'tensor'), may hold values from -24 to 24
- gate_bucket: bfloat16 [8192, 512], P(None, 'tensor'), may hold values from -0.0625 to 0.0625
- up_bucket: bfloat16 [8192, 512], P(None, 'tensor'), may hold values from -0.0625 to 0.0625
- down_bucket: bfloat16 [512, 8192], P('tensor'), may hold values from -0.03125 to 0.03125
Outputs:
- grad_proj: float32 [128, 4, 4096], P(None, 'tensor', 'dp')
- grad_gate: float32 [512, 8192], P('tensor', 'dp')
- grad_up: float32 [512, 8192], P('tensor', 'dp')
The draws below stay inside these ranges and needn't reach their ends.
Inputs may be any that keep to these rules, and one draw needn't show every extreme that they name: `row_map`: a permutation of the token ids; token id t belongs to student group t // 128; the rows of one device (aligned blocks of 128) send exactly 1 row to every student group.
All inputs are finite; a program needn't handle non-finite values.
Results may differ from the reference program's by a relative error of at most 0.0042.
Values may be sent and summed in bfloat16 or wider, within the bound.
A program may use at most 128 MiB of HBM per device.

```python
import jax
import jax.numpy as jnp
from jax import lax

DS = 8192
DT = 16384
FF = 28672
TOK_DEV = 128
HB = 512
PB = 128
TOKENS = 16384
N_TENSOR = 4


def draw_row_map(key, part):
    key = jax.random.fold_in(key, 7)
    groups = TOKENS // TOK_DEV
    per_peer = TOK_DEV // groups
    first_key, second_key = jax.random.split(key)
    slot_perm = jax.vmap(lambda k: jax.random.permutation(k, TOK_DEV))(jax.random.split(first_key, groups))
    arranged = jax.vmap(lambda k: jax.random.permutation(k, TOK_DEV))(jax.random.split(second_key, groups))
    group_ids = arranged // per_peer
    offset = arranged % per_peer
    sources = jnp.arange(groups, dtype=jnp.int32)[:, None]
    slots = slot_perm[group_ids, sources * per_peer + offset]
    return (group_ids * TOK_DEV + slots).reshape(-1).astype(jnp.int32)


def with_spikes(array, stream_key, source, target, shards_of, factor):
    owner, partner = [(jnp.arange(array.shape[axis_at]) // (array.shape[axis_at] // shards_of)).reshape([-1 if axis == axis_at else 1 for axis in range(array.ndim)]) for axis_at in (source, target)]
    chosen = jax.random.permutation(stream_key, shards_of)[partner]
    strong = (owner == chosen) | (owner == (partner + shards_of // 2) % shards_of)
    return jnp.where(strong, factor * array, array)


def block_scale(key, extent, cuts, low, top_value):
    loudness, own = 1.0, jax.random.fold_in(key, 6)
    for axis_at, parts in cuts:
        heights = jnp.exp(jax.random.uniform(jax.random.fold_in(own, axis_at), (parts,), jnp.float32, low / len(cuts), top_value / len(cuts)))
        loudness = loudness * jnp.repeat(heights, extent[axis_at] // parts).reshape([-1 if axis == axis_at else 1 for axis in range(len(extent))])
    return loudness


def bell_draw(stream_key, shape, width, bound, cuts=(), kind=jnp.bfloat16):
    result = jax.random.normal(stream_key, shape, jnp.float32) * width
    if len(cuts) > 0:
        result = block_scale(stream_key, shape, cuts, -0.22, 0.18) * result
    return jnp.clip(result, min=-bound, max=bound).astype(kind)


def noise_with(rng, extent, width, most, shards, heavy, kind=jnp.bfloat16):
    entries = width * jax.random.normal(rng, extent, jnp.float32)
    if shards:
        entries = entries * block_scale(rng, extent, shards, -0.22, 0.18)
    return jnp.clip(with_spikes(entries, jax.random.fold_in(rng, 3), *heavy), -most, most).astype(kind)


def setup_inputs(seed: int = 0) -> dict:
    key_list = jax.random.split(jax.random.key(seed), 9)
    return {
        "teacher_rows": noise_with(key_list[0], (TOKENS, DT), 1.0, 24.0, ((0, 128), (1, 4)), (0, 1, 128, 5.5)),
        "row_map": draw_row_map(jax.random.fold_in(key_list[8], 71), 0),
        "student_hidden": bell_draw(key_list[2], (TOKENS, DS), 1.0, 6.0, ((0, 128), (1, 4))),
        "projected": bell_draw(key_list[3], (TOKENS, DS), 1.0, 6.0, ((0, 128), (1, 4))),
        "mlp_input": noise_with(key_list[4], (TOKENS, DS), 1.0, 24.0, ((0, 128), (1, 4)), (0, 1, 128, 5.5)),
        "gate_bucket": bell_draw(key_list[5], (DS, HB), DS ** -0.5, 0.0625, ((1, 4),)),
        "up_bucket": bell_draw(key_list[6], (DS, HB), DS ** -0.5, 0.0625, ((1, 4),)),
        "down_bucket": bell_draw(key_list[7], (HB, DS), FF ** -0.5, 0.03125, ((0, 4),)),
    }


def reference(teacher_rows, row_map, student_hidden, projected, mlp_input, gate_bucket, up_bucket, down_bucket):
    handed = jnp.zeros((TOKENS, DT), jnp.bfloat16).at[row_map].set(teacher_rows)
    factor = float(TOKENS) ** -0.5
    err = ((student_hidden.astype(jnp.float32) - projected.astype(jnp.float32)) * factor).astype(jnp.bfloat16)
    proj_full = lax.dot_general(err[:, :PB], handed, (((0,), (0,)), ((), ())), preferred_element_type=jnp.float32)
    grad_proj = proj_full.reshape(PB, N_TENSOR, DT // N_TENSOR)
    act_grad = lax.dot_general(err, down_bucket, (((1,), (1,)), ((), ())), preferred_element_type=jnp.float32)
    gate_pre = jnp.dot(mlp_input, gate_bucket, preferred_element_type=jnp.float32)
    up_pre = jnp.dot(mlp_input, up_bucket, preferred_element_type=jnp.float32)
    sigmoid_gate = jax.nn.sigmoid(gate_pre)
    gate_grad = (act_grad * up_pre * sigmoid_gate * (1.0 + gate_pre * (1.0 - sigmoid_gate))).astype(jnp.bfloat16)
    up_grad = (act_grad * gate_pre * sigmoid_gate).astype(jnp.bfloat16)
    grad_gate = lax.dot_general(gate_grad, mlp_input, (((0,), (0,)), ((), ())), preferred_element_type=jnp.float32)
    grad_up = lax.dot_general(up_grad, mlp_input, (((0,), (0,)), ((), ())), preferred_element_type=jnp.float32)
    return (grad_proj, grad_gate, grad_up)
```

```python
import functools

import jax
import jax.numpy as jnp
from jax import lax
from jax.experimental import pallas as pl
from jax.experimental.pallas import tpu as pltpu
from jax.sharding import PartitionSpec as P

MESH = pl.DeviceIdType.MESH
BF = jnp.bfloat16
F32 = jnp.float32
NC = 2
HALVES = 2


def sizes(mesh, pb):
    nt = mesh.shape["tensor"]
    rest = mesh.shape["dp"] // (nt * NC)
    nx = 4 if rest == 16 else 2
    return dict(NY=nt, NZ=rest // nx, NX=nx, NT=nt, PB=pb)


def kernel(
    dims, teacher, rowmap, student, projected, mlp, gate, up, down, out,
    Xs, stu, prj, err, wgu, WdS, tea, TT, TA, XA, XT, G, E, pre, actp, actr, eb,
    RM, S0, S1, S2, S3, S4, msg, RB,
    ld, z_s, z_r, wd_s, wd_r, eb_s, eb_r, rm_s, rm_r, ea_s, ea_r, ea_l, xa_s, xa_r, ta_s, ta_r,
    act_s, act_r, e_s, e_r, g_s, g_r, rb_s, rb_r,
):
    NY, NZ, NX, NT, PB = (dims[k] for k in ("NY", "NZ", "NX", "NT", "PB"))
    NJ = NZ // NC
    TOK, S = mlp.shape
    H = gate.shape[1]
    DP = NY * NZ * NX * NC
    DTs = teacher.shape[1]
    L = S // (NZ * NX)
    LT = DTs // (NY * NZ * NX)
    NB = NY * NC * NX
    d = lax.axis_index("dp")
    t = lax.axis_index("tensor")
    c = lax.rem(d, NC)
    x = lax.rem(lax.div(d, NC), NX)
    zh = lax.rem(lax.div(d, NC * NX), NZ)
    y = lax.div(d, NC * NX * NZ)
    b = (y * NC + c) * NX + x
    factor = float(TOK * DP) ** -0.5
    drains = []

    def did(y_, zh_, x_, c_, t_):
        return (((y_ * NZ + zh_) * NX + x_) * NC + c_, t_)

    def send(src, dst, ssem, rsem, where):
        copy = pltpu.make_async_remote_copy(
            src_ref=src, dst_ref=dst, send_sem=ssem, recv_sem=rsem, device_id=where, device_id_type=MESH
        )
        copy.start()
        drains.append((None, copy))

    def send_if(cond, src, dst, ssem, rsem, where):
        @pl.when(cond)
        def _():
            pltpu.make_async_remote_copy(
                src_ref=src(), dst_ref=dst(), send_sem=ssem, recv_sem=rsem, device_id=where, device_id_type=MESH
            ).start()

    def arrived(ref, sem):
        pltpu.make_async_copy(ref, ref, sem).wait()

    def al(v, m):
        return pl.multiple_of(v, m)

    half = TOK // HALVES

    def rows_of(h):
        return pl.ds(h * half, half)

    loads = [
        pltpu.make_async_copy(rowmap, RM.at[y, zh, x, c], ld.at[0]),
        pltpu.make_async_copy(student, stu, ld.at[1]),
        pltpu.make_async_copy(projected, prj, ld.at[2]),
        pltpu.make_async_copy(mlp, Xs.at[t], ld.at[3]),
        pltpu.make_async_copy(teacher, tea, ld.at[4]),
        pltpu.make_async_copy(gate, wgu.at[:, pl.ds(0, H)], ld.at[5]),
        pltpu.make_async_copy(up, wgu.at[:, pl.ds(H, H)], ld.at[6]),
        pltpu.make_async_copy(down.at[:, pl.ds(al(t * S, S), S)], WdS.at[t], ld.at[7]),
    ]
    for copy in loads:
        copy.start()

    barrier = pltpu.get_barrier_semaphore()

    def greet(q, carry):
        q_x = lax.rem(q, NX)
        q_c = lax.rem(lax.div(q, NX), NC)
        q_y = lax.div(q, NX * NC)

        @pl.when(q != b)
        def _():
            pl.semaphore_signal(barrier, inc=1, device_id=did(q_y, zh, q_x, q_c, t), device_id_type=MESH)

        return carry

    lax.fori_loop(0, NB, greet, 0)
    for o in range(1, NZ):
        for q_c in range(NC):
            pl.semaphore_signal(
                barrier, inc=1, device_id=did(y, lax.rem(zh + o, NZ), x, q_c, t), device_id_type=MESH
            )
    for o in range(1, NT):
        pl.semaphore_signal(barrier, inc=1, device_id=(d, lax.rem(t + o, NT)), device_id_type=MESH)
    pl.semaphore_wait(barrier, NB - 1 + (NZ - 1) * NC + NT - 1)

    def z_send(k, h):
        sr, sl = t - k, t + k
        rows = rows_of(h)
        src_r = (lambda: mlp.at[rows]) if k == 0 else (lambda: Xs.at[sr, rows])
        src_l = (lambda: mlp.at[rows]) if k == 0 else (lambda: Xs.at[sl, rows])
        send_if((sr >= 0) & (t < NT - 1), src_r, lambda: Xs.at[sr, rows], z_s.at[0, k, h], z_r.at[0, k, h], (d, t + 1))
        send_if((sl <= NT - 1) & (t > 0), src_l, lambda: Xs.at[sl, rows], z_s.at[1, k, h], z_r.at[1, k, h], (d, t - 1))

    def z_drain(k, h):
        sr, sl = t - k, t + k

        @pl.when((sr >= 0) & (t < NT - 1))
        def _():
            arrived(Xs.at[sr, rows_of(h)], z_s.at[0, k, h])

        @pl.when((sl <= NT - 1) & (t > 0))
        def _():
            arrived(Xs.at[sl, rows_of(h)], z_s.at[1, k, h])

    def z_wait(k, h):
        @pl.when(t - k - 1 >= 0)
        def _():
            arrived(Xs.at[t - k - 1, rows_of(h)], z_r.at[0, k, h])

        @pl.when(t + k + 1 <= NT - 1)
        def _():
            arrived(Xs.at[t + k + 1, rows_of(h)], z_r.at[1, k, h])

    def a2a(s):
        def one(q, carry):
            q_x, q_c = lax.div(q, NC), lax.rem(q, NC)
            own = (s == y) & (q_x == x) & (q_c == c)
            for j in range(NJ):
                src = Xs.at[s, :, pl.ds(al(((q_c * NJ + j) * NX + q_x) * L, L), L)]
                dst = XA.at[pl.ds(al(b * TOK, TOK), TOK), pl.ds(j * L, L)]

                @pl.when(own)
                def _():
                    pltpu.make_async_copy(src, dst, xa_r).start()

                @pl.when(jnp.logical_not(own))
                def _():
                    pltpu.make_async_remote_copy(
                        src_ref=src, dst_ref=dst, send_sem=xa_s, recv_sem=xa_r,
                        device_id=did(s, zh, q_x, q_c, t), device_id_type=MESH,
                    ).start()

            return carry

        lax.fori_loop(0, NX * NC, one, 0)

    def add_pre(s):
        pre[...] += jnp.dot(Xs[s], wgu[pl.ds(al(s * S, S), S), :], preferred_element_type=F32)

    def consume(k):
        @pl.when(t - k - 1 >= 0)
        def _():
            a2a(t - k - 1)

        @pl.when(t + k + 1 <= NT - 1)
        def _():
            a2a(t + k + 1)

        @pl.when(t - k - 1 >= 0)
        def _():
            add_pre(t - k - 1)

        @pl.when(t + k + 1 <= NT - 1)
        def _():
            add_pre(t + k + 1)

    for h in range(HALVES):
        z_send(0, h)

    HR = H // (NX * NC)
    wrow = pl.ds(al((c * NX + x) * HR, HR), HR)
    for o in range(1, NT):
        p = lax.rem(t + o, NT)
        send(down.at[wrow, pl.ds(al(p * S, S), S)], WdS.at[t, wrow], wd_s.at[0, o - 1], wd_r.at[0, o - 1], (d, p))

    loads[0].wait()
    send(RM.at[y, zh, x, c], RM.at[y, zh, x, c], rm_s.at[0], rm_r.at[0, 0], did(y, zh, x, 1 - c, t))

    loads[1].wait()
    loads[2].wait()

    def err_rows(i, carry):
        r = pl.ds(al(i * 16, 16), 16)
        err[r, :] = ((stu[r, :].astype(F32) - prj[r, :].astype(F32)) * factor).astype(BF)
        return carry

    lax.fori_loop(0, TOK // 16, err_rows, 0)

    @pl.when(t == 0)
    def _():
        eb[...] = err[:, 0:PB]

    for o in range(1, NT):
        send_if(t == 0, lambda: eb, lambda: eb, eb_s.at[o - 1], eb_r, (d, o))

    loads[3].wait()
    a2a(t)

    arrived(RM.at[y, zh, x, 1 - c], rm_r.at[0, 0])
    for o in range(1, NX):
        q = lax.rem(x + o, NX)
        send(RM.at[y, zh, x], RM.at[y, zh, x], rm_s.at[1], rm_r.at[1, o - 1], did(y, zh, q, c, t))

    loads[4].wait()
    TC = DTs // 8

    def flip(i, carry):
        TT[pl.ds(al(i * TC, TC), TC), :] = jnp.transpose(tea[:, pl.ds(al(i * TC, TC), TC)])
        return carry

    lax.fori_loop(0, 4, flip, 0)

    for o in range(1, NX):
        arrived(RM.at[y, zh, lax.rem(x + NX - o, NX)], rm_r.at[1, o - 1])
    for o in range(1, NY):
        send(RM.at[y, zh], RM.at[y, zh], rm_s.at[2], rm_r.at[2, o - 1], did(lax.rem(y + o, NY), zh, x, c, t))

    for o in range(1, NT):
        p = lax.rem(t + NT - o, NT)
        arrived(WdS.at[p, wrow], wd_r.at[0, o - 1])
    for o in range(1, NT):
        p = lax.rem(t + NT - o, NT)
        for u in range(1, NX):
            send(
                WdS.at[p, wrow], WdS.at[p, wrow], wd_s.at[1, o - 1], wd_r.at[1, (o - 1) * (NX - 1) + u - 1],
                did(y, zh, lax.rem(x + u, NX), c, t),
            )

    lax.fori_loop(4, 8, flip, 0)

    for o in range(1, NY):
        arrived(RM.at[lax.rem(y + NY - o, NY), zh], rm_r.at[2, o - 1])
    for o in range(1, NZ):
        send(RM.at[:, zh], RM.at[:, zh], rm_s.at[3], rm_r.at[3, o - 1], did(y, lax.rem(zh + o, NZ), x, c, t))

    loads[5].wait()
    loads[6].wait()
    loads[7].wait()
    pre[...] = jnp.dot(Xs[t], wgu[pl.ds(al(t * S, S), S), :], preferred_element_type=F32)

    for o in range(1, NZ):
        arrived(RM.at[:, lax.rem(zh + NZ - o, NZ)], rm_r.at[3, o - 1])

    @pl.when(t != 0)
    def _():
        arrived(eb, eb_r)

    ids = RM[...].reshape(DP, TOK)
    slot = jnp.sum(jnp.where(lax.div(ids, TOK) == d, lax.rem(ids, TOK), 0), axis=1, keepdims=True)
    pick = (lax.broadcasted_iota(jnp.int32, (DP, TOK), 1) == slot).astype(F32).astype(BF)
    S0[...] = jnp.dot(pick, eb[...], preferred_element_type=F32).reshape(S0.shape)
    keep = [pltpu.make_async_copy(S0.at[y], S1.at[y], ea_l.at[0])]
    keep[0].start()
    for o in range(1, NY):
        q = lax.rem(y + o, NY)
        send(S0.at[q], S1.at[y], ea_s.at[0], ea_r.at[0, o - 1], did(q, zh, x, c, t))

    def z_step(k):
        for h in range(HALVES):
            z_wait(k, h)
            if k + 1 < NT - 1:
                z_send(k + 1, h)
        consume(k)

    if NT > 1:
        z_step(0)

    for o in range(1, NT):
        p = lax.rem(t + NT - o, NT)
        for u in range(1, NX):
            r = pl.ds(al((c * NX + lax.rem(x + NX - u, NX)) * HR, HR), HR)
            arrived(WdS.at[p, r], wd_r.at[1, (o - 1) * (NX - 1) + u - 1])
    crow = pl.ds(al(c * NX * HR, NX * HR), NX * HR)
    orow = pl.ds(al((1 - c) * NX * HR, NX * HR), NX * HR)
    for o in range(1, NT):
        p = lax.rem(t + NT - o, NT)
        send(WdS.at[p, crow], WdS.at[p, crow], wd_s.at[2, o - 1], wd_r.at[2, o - 1], did(y, zh, x, 1 - c, t))

    keep[0].wait()
    for o in range(1, NY):
        arrived(S1.at[lax.rem(y + NY - o, NY)], ea_r.at[0, o - 1])
    keep.append(pltpu.make_async_copy(S1.at[:, zh], S2.at[:, zh], ea_l.at[1]))
    keep[1].start()
    for o in range(1, NZ):
        q = lax.rem(zh + o, NZ)
        send(S1.at[:, q], S2.at[:, zh], ea_s.at[1], ea_r.at[1, o - 1], did(y, q, x, c, t))

    def tea_out(q, carry):
        q_x = lax.rem(q, NX)
        q_c = lax.rem(lax.div(q, NX), NC)
        q_y = lax.div(q, NX * NC)
        for j in range(NJ):
            src = TT.at[pl.ds(al(((q_y * NZ + q_c * NJ + j) * NX + q_x) * LT, LT), LT), :]
            dst = TA.at[pl.ds(j * LT, LT), pl.ds(al(b * TOK, TOK), TOK)]

            @pl.when(q == b)
            def _():
                pltpu.make_async_copy(src, dst, ta_r).start()

            @pl.when(q != b)
            def _():
                pltpu.make_async_remote_copy(
                    src_ref=src, dst_ref=dst, send_sem=ta_s, recv_sem=ta_r,
                    device_id=did(q_y, zh, q_x, q_c, t), device_id_type=MESH,
                ).start()

        return carry

    lax.fori_loop(0, NB, tea_out, 0)

    for o in range(1, NT):
        p = lax.rem(t + NT - o, NT)
        arrived(WdS.at[p, orow], wd_r.at[2, o - 1])
    for p in range(NT):
        actp[p] = lax.dot_general(err[...], WdS[p], (((1,), (1,)), ((), ())), preferred_element_type=F32)
    for o in range(1, NT):
        p = lax.rem(t + o, NT)
        send(actp.at[p], actr.at[o - 1], act_s.at[o - 1], act_r.at[o - 1], (d, p))

    keep[1].wait()
    for o in range(1, NZ):
        arrived(S2.at[:, lax.rem(zh + NZ - o, NZ)], ea_r.at[1, o - 1])
    keep.append(pltpu.make_async_copy(S2.at[:, :, x], S3.at[:, :, x], ea_l.at[2]))
    keep[2].start()
    for o in range(1, NX):
        q = lax.rem(x + o, NX)
        send(S2.at[:, :, q], S3.at[:, :, x], ea_s.at[2], ea_r.at[2, o - 1], did(y, zh, q, c, t))

    if NT > 2:
        z_step(1)

    keep[2].wait()
    for o in range(1, NX):
        arrived(S3.at[:, :, lax.rem(x + NX - o, NX)], ea_r.at[2, o - 1])
    keep.append(pltpu.make_async_copy(S3.at[:, :, :, c], S4.at[:, :, :, c], ea_l.at[3]))
    keep[3].start()
    send(S3.at[:, :, :, 1 - c], S4.at[:, :, :, c], ea_s.at[3], ea_r.at[3, 0], did(y, zh, x, 1 - c, t))
    keep[3].wait()
    arrived(S4.at[:, :, :, 1 - c], ea_r.at[3, 0])

    brow = pl.ds(al(b * TOK, TOK), TOK)

    def block(q_y, q_c, q_x):
        return pl.ds(al(((q_y * NC + q_c) * NX + q_x) * TOK, TOK), TOK)

    def group(q_y, q_c):
        return pl.ds(al((q_y * NC + q_c) * NX * TOK, NX * TOK), NX * TOK)

    mine = RM[y, zh, x, c]
    order = (lax.broadcasted_iota(jnp.int32, (DP, TOK), 0) == lax.div(mine, TOK)).astype(F32).astype(BF)
    E[brow, :] = lax.dot_general(
        order, S4[...].reshape(DP, PB).astype(BF), (((0,), (0,)), ((), ())), preferred_element_type=F32
    ).astype(BF)
    for o in range(1, NX):
        send(E.at[brow], E.at[brow], e_s.at[0], e_r.at[0, o - 1], did(y, zh, lax.rem(x + o, NX), c, t))
    for o in range(1, NX):
        arrived(E.at[block(y, c, lax.rem(x + NX - o, NX))], e_r.at[0, o - 1])
    for o in range(1, NY):
        send(E.at[group(y, c)], E.at[group(y, c)], e_s.at[1], e_r.at[1, o - 1], did(lax.rem(y + o, NY), zh, x, c, t))

    if NT > 3:
        z_step(2)

    for o in range(1, NY):
        arrived(E.at[group(lax.rem(y + NY - o, NY), c)], e_r.at[1, o - 1])
    for q_y in range(NY):
        send(E.at[group(q_y, c)], E.at[group(q_y, c)], e_s.at[2], e_r.at[2, q_y], did(y, zh, x, 1 - c, t))

    act = actp[t]
    for o in range(1, NT):
        arrived(actr.at[o - 1], act_r.at[o - 1])
        act = act + actr[o - 1]
    gate_pre, up_pre = pre[:, 0:H], pre[:, H : 2 * H]
    sig = jax.nn.sigmoid(gate_pre)
    G[brow, 0:H] = (act * up_pre * sig * (1.0 + gate_pre * (1.0 - sig))).astype(BF)
    G[brow, H : 2 * H] = (act * gate_pre * sig).astype(BF)
    lo, hi = pl.ds(0, H), pl.ds(H, H)
    for o in range(1, NX):
        send(G.at[brow, lo], G.at[brow, lo], g_s.at[0], g_r.at[0, o - 1], did(y, zh, lax.rem(x + o, NX), c, t))
    for o in range(1, NY):
        send(G.at[brow, hi], G.at[brow, hi], g_s.at[1], g_r.at[1, o - 1], did(lax.rem(y + o, NY), zh, x, c, t))
    for o in range(1, NX):
        arrived(G.at[block(y, c, lax.rem(x + NX - o, NX)), lo], g_r.at[0, o - 1])
    for o in range(1, NY):
        send(
            G.at[group(y, c), lo], G.at[group(y, c), lo], g_s.at[2], g_r.at[2, o - 1],
            did(lax.rem(y + o, NY), zh, x, c, t),
        )
    for o in range(1, NY):
        arrived(G.at[block(lax.rem(y + NY - o, NY), c, x), hi], g_r.at[1, o - 1])
    for o in range(1, NX):
        for q_y in range(NY):
            send(
                G.at[block(q_y, c, x), hi], G.at[block(q_y, c, x), hi], g_s.at[3],
                g_r.at[3, (o - 1) * NY + q_y], did(y, zh, lax.rem(x + o, NX), c, t),
            )

    arrived(XA, xa_r)
    CH = NB * TOK // 8

    def flip_x(i, carry):
        XT[:, pl.ds(al(i * CH, CH), CH)] = jnp.transpose(XA[pl.ds(al(i * CH, CH), CH), :])
        return carry

    lax.fori_loop(0, 8, flip_x, 0)

    for o in range(1, NY):
        arrived(G.at[group(lax.rem(y + NY - o, NY), c), lo], g_r.at[2, o - 1])
    for o in range(1, NX):
        for q_y in range(NY):
            arrived(G.at[block(q_y, c, lax.rem(x + NX - o, NX)), hi], g_r.at[3, (o - 1) * NY + q_y])
    for q_y in range(NY):
        send(G.at[group(q_y, c)], G.at[group(q_y, c)], g_s.at[4], g_r.at[4, q_y], did(y, zh, x, 1 - c, t))

    for q_y in range(NY):
        arrived(E.at[group(q_y, 1 - c)], e_r.at[2, q_y])
    arrived(TA, ta_r)
    proj = jnp.dot(TA[...], E[...], preferred_element_type=F32)
    KG = NX * TOK

    def part(q_y, q_c):
        at = al((q_y * NC + q_c) * KG, KG)
        return jnp.dot(XT[:, pl.ds(at, KG)], G[pl.ds(at, KG), :], preferred_element_type=F32)

    total = part(0, c)
    for q_y in range(1, NY):
        total = total + part(q_y, c)
    for q_y in range(NY):
        arrived(G.at[group(q_y, 1 - c)], g_r.at[4, q_y])
        total = total + part(q_y, 1 - c)

    R, RP = L // NC, LT // NC
    for j in range(NJ):
        for q_c in range(NC):
            at = j * L + q_c * R
            msg[j, q_c, 0:R, :] = total[at : at + R, 0:H].astype(BF)
            msg[j, q_c, R : 2 * R, :] = total[at : at + R, H : 2 * H].astype(BF)
            at = j * LT + q_c * RP
            msg[j, q_c, 2 * R : 2 * R + RP, :] = proj[at : at + RP, :].astype(BF)
    for j in range(NJ):
        q_z = c * NJ + j
        for q_c in range(NC):
            own = (q_z == zh) & (c == q_c)

            @pl.when(own)
            def _():
                pltpu.make_async_copy(msg.at[j, q_c], RB.at[zh], rb_r.at[zh]).start()

            send_if(
                jnp.logical_not(own), lambda: msg.at[j, q_c], lambda: RB.at[zh], rb_s.at[j, q_c], rb_r.at[zh],
                did(y, q_z, x, q_c, t),
            )
    for q in range(NZ):
        arrived(RB.at[q], rb_r.at[q])
    result = RB[0].astype(F32)
    for q in range(1, NZ):
        result = result + RB[q].astype(F32)
    out[...] = result

    for _, copy in drains:
        copy.wait_send()
    for k in range(NT - 1):
        for h in range(HALVES):
            z_drain(k, h)
    for o in range(1, NT):
        @pl.when(t == 0)
        def _():
            arrived(eb, eb_s.at[o - 1])
    for j in range(NJ):
        for q_c in range(NC):
            @pl.when(jnp.logical_not((c * NJ + j == zh) & (c == q_c)))
            def _():
                arrived(msg.at[j, q_c], rb_s.at[j, q_c])

    def drain_a2a(q, carry):
        for j in range(NJ):
            arrived(XA.at[pl.ds(0, TOK), pl.ds(j * L, L)], xa_s)
            arrived(TA.at[pl.ds(j * LT, LT), pl.ds(0, TOK)], ta_s)
        return carry

    lax.fori_loop(0, NB - 1, drain_a2a, 0)


def solution(mesh, pb=128):
    dims = sizes(mesh, pb)
    NY, NZ, NX, NT = (dims[k] for k in ("NY", "NZ", "NX", "NT"))

    def body(teacher_rows, row_map, student_hidden, projected, mlp_input, gate_bucket, up_bucket, down_bucket):
        TOK, S = mlp_input.shape
        F, H = gate_bucket.shape
        DTs = teacher_rows.shape[1]
        NJ = NZ // NC
        L, LT = S // (NZ * NX), DTs // (NY * NZ * NX)
        NB = NY * NC * NX
        R, RP = L // NC, LT // NC
        V, D = pltpu.VMEM, pltpu.SemaphoreType.DMA
        rows5 = (NY, NZ, NX, NC, 1, TOK)
        scratch = [
            V((NT, TOK, S), BF), V((TOK, S), BF), V((TOK, S), BF), V((TOK, S), BF),
            V((F, 2 * H), BF), V((NT, H, S), BF),
            V((TOK, DTs), BF), V((DTs, TOK), BF), V((NJ * LT, NB * TOK), BF),
            V((NB * TOK, NJ * L), BF), V((NJ * L, NB * TOK), BF),
            V((NB * TOK, 2 * H), BF), V((NB * TOK, pb), BF),
            V((TOK, 2 * H), F32), V((NT, TOK, H), F32), V((NT - 1, TOK, H), F32), V((TOK, pb), BF),
            V(rows5, jnp.int32),
        ]
        scratch += [V((NY, NZ, NX, NC, 1, pb), F32)] * 5
        scratch += [V((NJ, NC, 2 * R + RP, H), BF), V((NZ, 2 * R + RP, H), BF)]
        K = NT - 1
        scratch += [
            D((8,)), D((2, K, HALVES)), D((2, K, HALVES)),
            D((3, K)), D((3, K * max(NX - 1, 1))),
            D((K,)), D,
            D((4,)), D((4, 3)), D((4,)), D((4, 3)), D((4,)),
            D, D, D, D,
            D((K,)), D((K,)),
            D((3,)), D((3, 4)), D((5,)), D((5, 12)),
            D((NJ, NC)), D((NZ,)),
        ]
        res = pl.pallas_call(
            functools.partial(kernel, dims),
            out_shape=jax.ShapeDtypeStruct((2 * R + RP, H), F32),
            in_specs=[pl.BlockSpec(memory_space=pl.ANY)] * 8,
            out_specs=pl.BlockSpec(memory_space=pltpu.VMEM),
            scratch_shapes=scratch,
            compiler_params=pltpu.CompilerParams(
                collective_id=0, has_side_effects=True, vmem_limit_bytes=48 * 1024 * 1024
            ),
        )(teacher_rows, row_map.reshape(1, TOK), student_hidden, projected, mlp_input, gate_bucket, up_bucket, down_bucket)
        return res[2 * R :].T[:, None, :], res[:R].T, res[R : 2 * R].T

    in_specs = (
        P("dp", "tensor"), P("dp"), P("dp", "tensor"), P("dp", "tensor"), P("dp", "tensor"),
        P(None, "tensor"), P(None, "tensor"), P("tensor", None),
    )
    out_specs = (P(None, "tensor", "dp"), P("tensor", "dp"), P("tensor", "dp"))
    return jax.shard_map(body, mesh=mesh, in_specs=in_specs, out_specs=out_specs, check_vma=False)
```

```python
import functools

import jax
import jax.numpy as jnp
from jax import lax
from jax.experimental import pallas as pl
from jax.experimental.pallas import tpu as pltpu
from jax.sharding import PartitionSpec as P

MESH = pl.DeviceIdType.MESH
BF = jnp.bfloat16
F32 = jnp.float32
NC = 2
NZ = 4
HALVES = 2
VMEM_LIMIT = 62 * 1024 * 1024


def sizes(mesh, pb):
    nt = mesh.shape["tensor"]
    return dict(NY=nt, NX=mesh.shape["dp"] // (nt * NZ * NC), NT=nt, PB=pb)


def kernel(
    dims, teacher, rowmap, student, projected, mlp, gate, up, down, out,
    Xs, stu, prj, err, wgu, WdS, TAy, TAx, XAy, XAx, GEy, GEx, pre, actp, actr, eb,
    RM, S0, S1, S2, msg1, msg2, RB1, RB2, fin, RB3,
    ld, z_s, z_r, wd_s, wd_r, eb_s, eb_r, rm_s, rm_r, rp_s, rp_r, ea_s, ea_r, ez_s, ez_r, ez_l,
    xa_s, xa_r, ta_s, ta_r, act_s, act_r, e_s, e_r, g_s, g_r, r1_s, r1_r, r2_s, r2_r, rb_s, rb_r,
):
    NY, NX, NT, PB = (dims[k] for k in ("NY", "NX", "NT", "PB"))
    NS = NY // NC
    TOK, S = mlp.shape
    H = gate.shape[1]
    DP = NY * NZ * NX * NC
    DTs = teacher.shape[1]
    ZW, ZT = S // NZ, DTs // (NY * NZ)
    L, LT = ZW // NX, ZT // NX
    R, RP = L // NC, LT // NC
    ROWS = 2 * R + RP
    NB = NY * NC * NX
    d = lax.axis_index("dp")
    t = lax.axis_index("tensor")
    c = lax.rem(d, NC)
    x = lax.rem(lax.div(d, NC), NX)
    zh = lax.rem(lax.div(d, NC * NX), NZ)
    y = lax.div(d, NC * NX * NZ)
    b = (y * NC + c) * NX + x
    factor = float(TOK * DP) ** -0.5
    shift = TOK.bit_length() - 1
    drains = []

    def did(y_, zh_, x_, c_, t_):
        return (((y_ * NZ + zh_) * NX + x_) * NC + c_, t_)

    def start(src, dst, ssem, rsem, where):
        copy = pltpu.make_async_remote_copy(
            src_ref=src, dst_ref=dst, send_sem=ssem, recv_sem=rsem, device_id=where, device_id_type=MESH
        )
        copy.start()
        return copy

    def send(src, dst, ssem, rsem, where):
        drains.append(start(src, dst, ssem, rsem, where))

    def send_if(cond, src, dst, ssem, rsem, where):
        @pl.when(cond)
        def _():
            start(src(), dst(), ssem, rsem, where)

    def arrived(ref, sem):
        pltpu.make_async_copy(ref, ref, sem).wait()

    def copy_or_send(own, src, dst, ssem, rsem, where):
        @pl.when(own)
        def _():
            pltpu.make_async_copy(src, dst, rsem).start()

        @pl.when(jnp.logical_not(own))
        def _():
            start(src, dst, ssem, rsem, where)

    def al(v, m):
        return pl.multiple_of(v, m)

    def plane(fn):
        def one(q, carry):
            fn(q, lax.div(q, NX * NC), lax.rem(q, NX), lax.rem(lax.div(q, NX), NC))
            return carry

        lax.fori_loop(0, NB, one, 0)

    half = TOK // HALVES

    def rows_of(h):
        return pl.ds(h * half, half)

    loads = [
        pltpu.make_async_copy(rowmap, RM.at[b, zh], ld.at[0]),
        pltpu.make_async_copy(student, stu, ld.at[1]),
        pltpu.make_async_copy(projected, prj, ld.at[2]),
        pltpu.make_async_copy(mlp, Xs.at[t], ld.at[3]),
        pltpu.make_async_copy(down.at[:, pl.ds(al(t * S, S), S)], WdS.at[t], ld.at[4]),
        pltpu.make_async_copy(gate, wgu.at[:, pl.ds(0, H)], ld.at[5]),
        pltpu.make_async_copy(up, wgu.at[:, pl.ds(H, H)], ld.at[6]),
    ]
    for copy in loads:
        copy.start()

    to_z = NC + lax.div(x * NC, NX)
    to_x = lax.rem(x * NC, NX) + c
    blk = (zh - NC) * NX + x
    from_x = jnp.where(zh < NC, x, lax.div(blk, NC))
    from_c = jnp.where(zh < NC, zh, lax.rem(blk, NC))

    barrier = pltpu.get_barrier_semaphore()

    def greet(where):
        pl.semaphore_signal(barrier, inc=1, device_id=where, device_id_type=MESH)

    def greet_plane(q, q_y, q_x, q_c):
        @pl.when(q != b)
        def _():
            greet(did(q_y, zh, q_x, q_c, t))

    plane(greet_plane)
    for o in range(1, NZ):
        greet(did(y, lax.rem(zh + o, NZ), x, c, t))
    for o in range(1, NT):
        greet((d, lax.rem(t + o, NT)))
    for q in range(NZ):
        @pl.when(jnp.logical_not((q == zh) & (from_x == x) & (from_c == c)))
        def _():
            greet(did(y, q, from_x, from_c, t))
    to_self = (c == zh) | ((to_z == zh) & (to_x == x))
    pl.semaphore_wait(barrier, NB - 1 + NZ - 1 + NT - 1 + 2 * NC - jnp.where(to_self, 1, 0))

    def z_send(k, h):
        sr, sl = t - k, t + k
        rows = rows_of(h)
        src_r = (lambda: mlp.at[rows]) if k == 0 else (lambda: Xs.at[sr, rows])
        src_l = (lambda: mlp.at[rows]) if k == 0 else (lambda: Xs.at[sl, rows])
        send_if((sr >= 0) & (t < NT - 1), src_r, lambda: Xs.at[sr, rows], z_s.at[0, k, h], z_r.at[0, k, h], (d, t + 1))
        send_if((sl <= NT - 1) & (t > 0), src_l, lambda: Xs.at[sl, rows], z_s.at[1, k, h], z_r.at[1, k, h], (d, t - 1))

    def z_drain(k, h):
        sr, sl = t - k, t + k

        @pl.when((sr >= 0) & (t < NT - 1))
        def _():
            arrived(Xs.at[sr, rows_of(h)], z_s.at[0, k, h])

        @pl.when((sl <= NT - 1) & (t > 0))
        def _():
            arrived(Xs.at[sl, rows_of(h)], z_s.at[1, k, h])

    def z_wait(k, h):
        @pl.when(t - k - 1 >= 0)
        def _():
            arrived(Xs.at[t - k - 1, rows_of(h)], z_r.at[0, k, h])

        @pl.when(t + k + 1 <= NT - 1)
        def _():
            arrived(Xs.at[t + k + 1, rows_of(h)], z_r.at[1, k, h])

    yrow = pl.ds(al((y * NC + c) * TOK, TOK), TOK)
    xrow = pl.ds(al((x * NC + c) * TOK, TOK), TOK)

    def a2a(s):
        for q_c in range(NC):
            copy_or_send(
                (s == y) & (q_c == c), Xs.at[s, :, pl.ds(q_c * ZW, ZW)], XAy.at[yrow], xa_s.at[0], xa_r.at[0],
                did(s, zh, x, q_c, t),
            )
        q_c = lax.div(s, NS)
        lane = pl.ds(al(lax.rem(s, NS) * NC * L, NC * L), NC * L)

        def one(q, carry):
            src = Xs.at[s, :, pl.ds(al((NX + q) * NC * L, NC * L), NC * L)]
            copy_or_send((q == x) & (q_c == c), src, XAx.at[xrow, lane], xa_s.at[1], xa_r.at[1], did(y, zh, q, q_c, t))
            return carry

        lax.fori_loop(0, NX, one, 0)

    def add_pre(s):
        pre[...] += jnp.dot(Xs[s], wgu[pl.ds(al(s * S, S), S), :], preferred_element_type=F32)

    def z_pass(k):
        for h in range(HALVES):
            z_wait(k, h)
            if k + 1 < NT - 1:
                z_send(k + 1, h)

        @pl.when(t - k - 1 >= 0)
        def _():
            a2a(t - k - 1)

        @pl.when(t + k + 1 <= NT - 1)
        def _():
            a2a(t + k + 1)

    def z_dot(k):
        @pl.when(t - k - 1 >= 0)
        def _():
            add_pre(t - k - 1)

        @pl.when(t + k + 1 <= NT - 1)
        def _():
            add_pre(t + k + 1)

    for h in range(HALVES):
        z_send(0, h)

    HR = H // (NX * NC)
    wrow = pl.ds(al((c * NX + x) * HR, HR), HR)
    crow = pl.ds(al(c * NX * HR, NX * HR), NX * HR)
    orow = pl.ds(al((1 - c) * NX * HR, NX * HR), NX * HR)
    for o in range(1, NT):
        p = lax.rem(t + o, NT)
        send(down.at[wrow, pl.ds(al(p * S, S), S)], WdS.at[t, wrow], wd_s.at[0, o - 1], wd_r.at[0, o - 1], (d, p))

    loads[0].wait()
    for o in range(1, NZ):
        q = lax.rem(zh + o, NZ)
        send(RM.at[b, zh], RM.at[b, zh], rm_s.at[o - 1], rm_r.at[o - 1], did(y, q, x, c, t))

    loads[1].wait()
    loads[2].wait()

    def err_rows(i, carry):
        r = pl.ds(al(i * 16, 16), 16)
        err[r, :] = ((stu[r, :].astype(F32) - prj[r, :].astype(F32)) * factor).astype(BF)
        return carry

    lax.fori_loop(0, TOK // 16, err_rows, 0)

    @pl.when(t == 0)
    def _():
        eb[...] = err[:, 0:PB]

    for o in range(1, NT):
        send_if(t == 0, lambda: eb, lambda: eb, eb_s.at[o - 1], eb_r, (d, o))

    for o in range(1, NZ):
        arrived(RM.at[b, lax.rem(zh + NZ - o, NZ)], rm_r.at[o - 1])

    def rm_out(q, q_y, q_x, q_c):
        @pl.when(q != b)
        def _():
            start(RM.at[b], RM.at[b], rp_s, rp_r, did(q_y, zh, q_x, q_c, t))

    plane(rm_out)

    for o in range(1, NT):
        p = lax.rem(t + NT - o, NT)
        arrived(WdS.at[p, wrow], wd_r.at[0, o - 1])
        for u in range(1, NX):
            send(
                WdS.at[p, wrow], WdS.at[p, wrow], wd_s.at[1, o - 1], wd_r.at[1, (o - 1) * (NX - 1) + u - 1],
                did(y, zh, lax.rem(x + u, NX), c, t),
            )

    loads[3].wait()
    a2a(t)

    loads[5].wait()
    loads[6].wait()
    pre[...] = jnp.dot(Xs[t], wgu[pl.ds(al(t * S, S), S), :], preferred_element_type=F32)

    if NT > 1:
        z_pass(0)

    arrived(RM.at[pl.ds(0, NB - 1)], rp_r)

    @pl.when(t != 0)
    def _():
        arrived(eb, eb_r)

    ids = RM[...].reshape(DP, TOK)
    slot = jnp.sum(jnp.where((ids >> shift) == d, ids & (TOK - 1), 0), axis=1, keepdims=True)
    pick = (lax.broadcasted_iota(jnp.int32, (DP, TOK), 1) == slot).astype(F32).astype(BF)
    S0[...] = jnp.dot(pick, eb[...], preferred_element_type=F32).reshape(S0.shape)

    def ea_out(q, q_y, q_x, q_c):
        copy_or_send(q == b, S0.at[q], S1.at[b], ea_s, ea_r, did(q_y, zh, q_x, q_c, t))

    plane(ea_out)

    for o in range(1, NT):
        p = lax.rem(t + NT - o, NT)
        for u in range(1, NX):
            r = pl.ds(al((c * NX + lax.rem(x + NX - u, NX)) * HR, HR), HR)
            arrived(WdS.at[p, r], wd_r.at[1, (o - 1) * (NX - 1) + u - 1])
        send(WdS.at[p, crow], WdS.at[p, crow], wd_s.at[2, o - 1], wd_r.at[2, o - 1], did(y, zh, x, 1 - c, t))

    if NT > 1:
        z_dot(0)
    if NT > 2:
        z_pass(1)

    arrived(S1, ea_r)
    keep = pltpu.make_async_copy(S1.at[:, zh], S2.at[:, zh], ez_l)
    keep.start()
    for o in range(1, NZ):
        q = lax.rem(zh + o, NZ)
        send(S1.at[:, q], S2.at[:, zh], ez_s.at[o - 1], ez_r.at[o - 1], did(y, q, x, c, t))

    loads[4].wait()
    for o in range(1, NT):
        p = lax.rem(t + NT - o, NT)
        arrived(WdS.at[p, orow], wd_r.at[2, o - 1])
    for p in range(NT):
        actp[p] = lax.dot_general(err[...], WdS[p], (((1,), (1,)), ((), ())), preferred_element_type=F32)
    for o in range(1, NT):
        p = lax.rem(t + o, NT)
        send(actp.at[p], actr.at[o - 1], act_s.at[o - 1], act_r.at[o - 1], (d, p))

    def tea_y(q, carry):
        q_y, q_c = lax.div(q, NC), lax.rem(q, NC)
        src = teacher.at[:, pl.ds(al((q_y * NZ + q_c) * ZT, ZT), ZT)]
        copy_or_send((q_y == y) & (q_c == c), src, TAy.at[yrow], ta_s.at[0], ta_r.at[0], did(q_y, zh, x, q_c, t))
        return carry

    def tea_x(q, carry):
        s, q_x = lax.div(q, NX), lax.rem(q, NX)
        q_c = lax.div(s, NS)
        src = teacher.at[:, pl.ds(al(((s * NZ + NC) * NX + q_x * NC) * LT, NC * LT), NC * LT)]
        dst = TAx.at[xrow, pl.ds(al(lax.rem(s, NS) * NC * LT, NC * LT), NC * LT)]
        copy_or_send((q_x == x) & (q_c == c), src, dst, ta_s.at[1], ta_r.at[1], did(y, zh, q_x, q_c, t))
        return carry

    lax.fori_loop(0, NY * NC, tea_y, 0)
    lax.fori_loop(0, NY * NX, tea_x, 0)

    if NT > 2:
        z_dot(1)
    if NT > 3:
        z_pass(2)

    keep.wait()
    for o in range(1, NZ):
        arrived(S2.at[:, lax.rem(zh + NZ - o, NZ)], ez_r.at[o - 1])
    row = lax.broadcasted_iota(jnp.int32, (DP, 1), 0)
    row_z, row_b = lax.rem(row, NZ), lax.div(row, NZ)
    row_x, row_c, row_y = lax.rem(row_b, NX), lax.rem(lax.div(row_b, NX), NC), lax.div(row_b, NX * NC)
    row_d = ((row_y * NZ + row_z) * NX + row_x) * NC + row_c
    order = ((RM[b, zh] >> shift) == row_d).astype(F32).astype(BF)
    sorted_err = lax.dot_general(
        S2[...].reshape(DP, PB).astype(BF), order, (((0,), (0,)), ((), ())), preferred_element_type=F32
    ).astype(BF)
    hid, proj_rows = pl.ds(0, 2 * H), pl.ds(2 * H, PB)
    GEy[proj_rows, yrow] = sorted_err
    GEx[proj_rows, xrow] = sorted_err

    def spread(rows, ssem, rsem):
        for q_c in range(NC):
            for o in range(1, NX):
                send(GEx.at[rows, xrow], GEx.at[rows, xrow], ssem.at[1], rsem.at[1], did(y, zh, lax.rem(x + o, NX), q_c, t))
            for o in range(1, NY):
                send(GEy.at[rows, yrow], GEy.at[rows, yrow], ssem.at[0], rsem.at[0], did(lax.rem(y + o, NY), zh, x, q_c, t))
        send(GEx.at[rows, xrow], GEx.at[rows, xrow], ssem.at[1], rsem.at[1], did(y, zh, x, 1 - c, t))
        send(GEy.at[rows, yrow], GEy.at[rows, yrow], ssem.at[0], rsem.at[0], did(y, zh, x, 1 - c, t))

    spread(proj_rows, e_s, e_r)

    if NT > 3:
        z_dot(2)

    act = actp[t]
    for o in range(1, NT):
        arrived(actr.at[o - 1], act_r.at[o - 1])
        act = act + actr[o - 1]
    gate_pre, up_pre = pre[:, 0:H], pre[:, H : 2 * H]
    sig = jax.nn.sigmoid(gate_pre)
    gate_grad = jnp.transpose(act * up_pre * sig * (1.0 + gate_pre * (1.0 - sig))).astype(BF)
    up_grad = jnp.transpose(act * gate_pre * sig).astype(BF)
    for buf, at in ((GEx, xrow), (GEy, yrow)):
        buf[0:H, at] = gate_grad
        buf[H : 2 * H, at] = up_grad
    spread(hid, g_s, g_r)

    oy, ox = pl.ds(0, (NY * NC - 1) * TOK), pl.ds(0, (NX * NC - 1) * TOK)
    arrived(GEy.at[proj_rows, oy], e_r.at[0])
    arrived(GEx.at[proj_rows, ox], e_r.at[1])
    arrived(TAy, ta_r.at[0])
    arrived(TAx, ta_r.at[1])
    proj1 = jnp.transpose(jnp.dot(GEy[proj_rows, :], TAy[...], preferred_element_type=F32)).astype(BF)
    proj2 = jnp.transpose(jnp.dot(GEx[proj_rows, :], TAx[...], preferred_element_type=F32)).astype(BF)
    for q in range(NX):
        msg1[q, 2 * H : 2 * H + LT, :] = proj1[q * LT : (q + 1) * LT, :]
    for i in range(NS):
        for q_c in range(NC):
            at = (i * NC + q_c) * LT
            msg2[i, q_c, 2 * H : 2 * H + LT, :] = proj2[at : at + LT, :]

    arrived(XAx, xa_r.at[1])
    arrived(GEx.at[hid, ox], g_r.at[1])
    tot2 = jnp.dot(GEx[hid, :], XAx[...], preferred_element_type=F32)
    for i in range(NS):
        for q_c in range(NC):
            at = (i * NC + q_c) * L
            msg2[i, q_c, 0 : 2 * H, 0:L] = tot2[:, at : at + L].astype(BF)
            s = c * NS + i
            copy_or_send(
                (s == y) & (q_c == c), msg2.at[i, q_c], RB2.at[y], r2_s.at[i, q_c], r2_r.at[y], did(s, zh, x, q_c, t)
            )
    arrived(XAy, xa_r.at[0])
    arrived(GEy.at[hid, oy], g_r.at[0])
    tot1 = jnp.dot(GEy[hid, :], XAy[...], preferred_element_type=F32)
    for q in range(NX):
        msg1[q, 0 : 2 * H, 0:L] = tot1[:, q * L : (q + 1) * L].astype(BF)
        copy_or_send(q == x, msg1.at[q], RB1.at[x], r1_s.at[q], r1_r.at[x], did(y, zh, q, c, t))

    for kind, (buf, sem, count, where) in enumerate(
        ((RB2, r2_r, NY, lambda q_c: (to_z, to_x, q_c)), (RB1, r1_r, NX, lambda q_c: (c, x, q_c)))
    ):
        part = None
        for q in range(count):
            arrived(buf.at[q], sem.at[q])
            part = buf[q].astype(F32) if part is None else part + buf[q].astype(F32)
        feats = jnp.transpose(part[0 : 2 * H, 0:L])
        for q_c in range(NC):
            r = slice(q_c * R, (q_c + 1) * R)
            fin[kind, q_c, 0:R, :] = feats[r, 0:H].astype(BF)
            fin[kind, q_c, R : 2 * R, :] = feats[r, H : 2 * H].astype(BF)
            at = 2 * H + q_c * RP
            fin[kind, q_c, 2 * R : ROWS, :] = part[at : at + RP, :].astype(BF)
            q_z, q_x, _ = where(q_c)
            copy_or_send(
                (q_z == zh) & (q_x == x) & (q_c == c), fin.at[kind, q_c], RB3.at[zh], rb_s.at[kind, q_c], rb_r.at[zh],
                did(y, q_z, q_x, q_c, t),
            )
    result = None
    for q in range(NZ):
        arrived(RB3.at[q], rb_r.at[q])
        result = RB3[q].astype(F32) if result is None else result + RB3[q].astype(F32)
    out[...] = result

    def left(own, ref, sem):
        @pl.when(jnp.logical_not(own))
        def _():
            arrived(ref, sem)

    for copy in drains:
        copy.wait_send()
    for k in range(NT - 1):
        for h in range(HALVES):
            z_drain(k, h)
    for o in range(1, NT):
        left(t != 0, eb, eb_s.at[o - 1])
    for q in range(NX):
        left(q == x, msg1.at[q], r1_s.at[q])
    for q_c in range(NC):
        for i in range(NS):
            left((c * NS + i == y) & (q_c == c), msg2.at[i, q_c], r2_s.at[i, q_c])
        left((to_z == zh) & (to_x == x) & (q_c == c), fin.at[0, q_c], rb_s.at[0, q_c])
        left((c == zh) & (q_c == c), fin.at[1, q_c], rb_s.at[1, q_c])
    arrived(RM.at[pl.ds(0, NB - 1)], rp_s)
    arrived(S1.at[pl.ds(0, NB - 1)], ea_s)
    for ref, sem, count in ((XAy, xa_s, NY), (TAy, ta_s, NY)):
        arrived(ref.at[pl.ds(0, (count * NC - 1) * TOK)], sem.at[0])
    for ref, sem, count in ((XAx, xa_s, NX), (TAx, ta_s, NX)):
        arrived(ref.at[pl.ds(0, (count * NC - 1) * TOK)], sem.at[1])


def solution(mesh, pb=128):
    dims = sizes(mesh, pb)
    NY, NX, NT = (dims[k] for k in ("NY", "NX", "NT"))

    def body(teacher_rows, row_map, student_hidden, projected, mlp_input, gate_bucket, up_bucket, down_bucket):
        TOK, S = mlp_input.shape
        F, H = gate_bucket.shape
        DTs = teacher_rows.shape[1]
        NS = NY // NC
        ZW, ZT = S // NZ, DTs // (NY * NZ)
        L, LT = ZW // NX, ZT // NX
        R, RP = L // NC, LT // NC
        NB = NY * NC * NX
        ROWS, MSG = 2 * R + RP, 2 * H + LT
        V, D = pltpu.VMEM, pltpu.SemaphoreType.DMA
        K = NT - 1
        scratch = [
            V((NT, TOK, S), BF), V((TOK, S), BF), V((TOK, S), BF), V((TOK, S), BF),
            V((F, 2 * H), BF), V((NT, H, S), BF),
            V((NY * NC * TOK, ZT), BF), V((NX * NC * TOK, NS * NC * LT), BF),
            V((NY * NC * TOK, ZW), BF), V((NX * NC * TOK, NS * NC * L), BF),
            V((2 * H + pb, NY * NC * TOK), BF), V((2 * H + pb, NX * NC * TOK), BF),
            V((TOK, 2 * H), F32), V((NT, TOK, H), F32), V((K, TOK, H), F32), V((TOK, pb), BF),
            V((NB, NZ, 1, TOK), jnp.int32), V((NB, NZ, 1, pb), F32), V((NB, NZ, 1, pb), F32), V((NB, NZ, 1, pb), F32),
            V((NX, MSG, H), BF), V((NS, NC, MSG, H), BF), V((NX, MSG, H), BF), V((NY, MSG, H), BF),
            V((2, NC, ROWS, H), BF), V((NZ, ROWS, H), BF),
            D((7,)), D((2, K, HALVES)), D((2, K, HALVES)),
            D((3, K)), D((3, K * max(NX - 1, 1))),
            D((K,)), D,
            D((NZ - 1,)), D((NZ - 1,)), D, D, D, D, D((NZ - 1,)), D((NZ - 1,)), D,
            D((2,)), D((2,)), D((2,)), D((2,)),
            D((K,)), D((K,)),
            D((2,)), D((2,)), D((2,)), D((2,)),
            D((NX,)), D((NX,)), D((NS, NC)), D((NY,)), D((2, NC)), D((NZ,)),
        ]
        res = pl.pallas_call(
            functools.partial(kernel, dims),
            out_shape=jax.ShapeDtypeStruct((2 * R + RP, H), F32),
            in_specs=[pl.BlockSpec(memory_space=pl.ANY)] * 8,
            out_specs=pl.BlockSpec(memory_space=pltpu.VMEM),
            scratch_shapes=scratch,
            compiler_params=pltpu.CompilerParams(
                collective_id=0, has_side_effects=True, vmem_limit_bytes=VMEM_LIMIT
            ),
        )(teacher_rows, row_map.reshape(1, TOK), student_hidden, projected, mlp_input, gate_bucket, up_bucket, down_bucket)
        return res[2 * R :].T[:, None, :], res[:R].T, res[R : 2 * R].T

    in_specs = (
        P("dp", "tensor"), P("dp"), P("dp", "tensor"), P("dp", "tensor"), P("dp", "tensor"),
        P(None, "tensor"), P(None, "tensor"), P("tensor", None),
    )
    out_specs = (P(None, "tensor", "dp"), P("tensor", "dp"), P("tensor", "dp"))
    return jax.shard_map(body, mesh=mesh, in_specs=in_specs, out_specs=out_specs, check_vma=False)
```

```python
import functools

import jax
import jax.numpy as jnp
from jax import lax
from jax.experimental import pallas as pl
from jax.experimental.pallas import tpu as pltpu
from jax.sharding import PartitionSpec as P

MESH = pl.DeviceIdType.MESH
BF = jnp.bfloat16
F32 = jnp.float32
NC = 2
NZ = 4
HALVES = 2
VMEM_LIMIT = 62 * 1024 * 1024


def sizes(mesh, pb):
    nt = mesh.shape["tensor"]
    return dict(NY=nt, NX=mesh.shape["dp"] // (nt * NZ * NC), NT=nt, PB=pb)


def kernel(
    dims, teacher, rowmap, student, projected, mlp, gate, up, down, out,
    Xs, stu, prj, err, wgu, WdS, TAy, XAy, XAx, GEy, GEx, pre, actp, actr, eb,
    RM, S0, S1, S2, S3, msg1, msg2, msgp, RB1, RB2, RBX, fin, finp, RB3, RBP,
    ld, z_s, z_r, wd_s, wd_r, eb_s, eb_r, rm_s, rm_r, ea_s, ea_r, ea_l,
    xa_s, xa_r, ta_s, ta_r, act_s, act_r, e_s, e_r, g_s, g_r, r1_s, r1_r, r2_s, r2_r, rq_s, rq_r, rb_s, rb_r, rp_s, rp_r,
):
    NY, NX, NT, PB = (dims[k] for k in ("NY", "NX", "NT", "PB"))
    NS = NY // NC
    TOK, S = mlp.shape
    H = gate.shape[1]
    DP = NY * NZ * NX * NC
    DTs = teacher.shape[1]
    ZW, ZT = S // NZ, DTs // (NY * NZ)
    L, LT = ZW // NX, ZT // NX
    R, RP = L // NC, LT // NC
    NP = NZ // NC
    d = lax.axis_index("dp")
    t = lax.axis_index("tensor")
    c = lax.rem(d, NC)
    x = lax.rem(lax.div(d, NC), NX)
    zh = lax.rem(lax.div(d, NC * NX), NZ)
    y = lax.div(d, NC * NX * NZ)
    factor = float(TOK * DP) ** -0.5
    shift = TOK.bit_length() - 1
    drains = []

    def did(y_, zh_, x_, c_, t_):
        return (((y_ * NZ + zh_) * NX + x_) * NC + c_, t_)

    def start(src, dst, ssem, rsem, where):
        copy = pltpu.make_async_remote_copy(
            src_ref=src, dst_ref=dst, send_sem=ssem, recv_sem=rsem, device_id=where, device_id_type=MESH
        )
        copy.start()
        return copy

    def send(src, dst, ssem, rsem, where):
        drains.append(start(src, dst, ssem, rsem, where))

    def send_if(cond, src, dst, ssem, rsem, where):
        @pl.when(cond)
        def _():
            start(src(), dst(), ssem, rsem, where)

    def arrived(ref, sem):
        pltpu.make_async_copy(ref, ref, sem).wait()

    def copy_or_send(own, src, dst, ssem, rsem, where):
        @pl.when(own)
        def _():
            pltpu.make_async_copy(src, dst, rsem).start()

        @pl.when(jnp.logical_not(own))
        def _():
            start(src, dst, ssem, rsem, where)

    def al(v, m):
        return pl.multiple_of(v, m)

    half = TOK // HALVES

    def rows_of(h):
        return pl.ds(h * half, half)

    loads = [
        pltpu.make_async_copy(rowmap, RM.at[y, zh, x, c], ld.at[0]),
        pltpu.make_async_copy(student, stu, ld.at[1]),
        pltpu.make_async_copy(projected, prj, ld.at[2]),
        pltpu.make_async_copy(mlp, Xs.at[t], ld.at[3]),
        pltpu.make_async_copy(down.at[:, pl.ds(al(t * S, S), S)], WdS.at[0], ld.at[4]),
        pltpu.make_async_copy(gate, wgu.at[:, pl.ds(0, H)], ld.at[5]),
        pltpu.make_async_copy(up, wgu.at[:, pl.ds(H, H)], ld.at[6]),
    ]
    for copy in loads:
        copy.start()

    to_z = NC + lax.div(x * NC, NX)
    to_x = lax.rem(x * NC, NX) + c
    blk = (zh - NC) * NX + x
    from_x = jnp.where(zh < NC, x, lax.div(blk, NC))
    from_c = jnp.where(zh < NC, zh, lax.rem(blk, NC))

    barrier = pltpu.get_barrier_semaphore()

    def greet(where):
        pl.semaphore_signal(barrier, inc=1, device_id=where, device_id_type=MESH)

    for q_c in range(NC):
        for o in range(1, NX):
            greet(did(y, zh, lax.rem(x + o, NX), q_c, t))
        for o in range(1, NY):
            greet(did(lax.rem(y + o, NY), zh, x, q_c, t))
    greet(did(y, zh, x, 1 - c, t))
    for o in range(1, NZ):
        greet(did(y, lax.rem(zh + o, NZ), x, c, t))
    for o in range(1, NT):
        greet((d, lax.rem(t + o, NT)))
    for q in range(NZ):
        @pl.when(jnp.logical_not((q == zh) & (from_x == x) & (from_c == c)))
        def _():
            greet(did(y, q, from_x, from_c, t))
        @pl.when(jnp.logical_not((q == zh) & (lax.div(zh, NP) == c)))
        def _():
            greet(did(y, q, x, lax.div(zh, NP), t))
    to_self = (c == zh) | ((to_z == zh) & (to_x == x))
    to_self_p = lax.div(zh, NP) == c
    pl.semaphore_wait(
        barrier,
        (NX - 1 + NY - 1) * NC + 1 + NZ - 1 + NT - 1 + 2 * NC + NP * NC
        - jnp.where(to_self, 1, 0) - jnp.where(to_self_p, 1, 0),
    )

    def z_send(k, h):
        sr, sl = t - k, t + k
        rows = rows_of(h)
        src_r = (lambda: mlp.at[rows]) if k == 0 else (lambda: Xs.at[sr, rows])
        src_l = (lambda: mlp.at[rows]) if k == 0 else (lambda: Xs.at[sl, rows])
        send_if((sr >= 0) & (t < NT - 1), src_r, lambda: Xs.at[sr, rows], z_s.at[0, k, h], z_r.at[0, k, h], (d, t + 1))
        send_if((sl <= NT - 1) & (t > 0), src_l, lambda: Xs.at[sl, rows], z_s.at[1, k, h], z_r.at[1, k, h], (d, t - 1))

    def z_drain(k, h):
        sr, sl = t - k, t + k

        @pl.when((sr >= 0) & (t < NT - 1))
        def _():
            arrived(Xs.at[sr, rows_of(h)], z_s.at[0, k, h])

        @pl.when((sl <= NT - 1) & (t > 0))
        def _():
            arrived(Xs.at[sl, rows_of(h)], z_s.at[1, k, h])

    def z_wait(k, h):
        @pl.when(t - k - 1 >= 0)
        def _():
            arrived(Xs.at[t - k - 1, rows_of(h)], z_r.at[0, k, h])

        @pl.when(t + k + 1 <= NT - 1)
        def _():
            arrived(Xs.at[t + k + 1, rows_of(h)], z_r.at[1, k, h])

    yrow = pl.ds(al((y * NC + c) * TOK, TOK), TOK)
    xrow = pl.ds(al((x * NC + c) * TOK, TOK), TOK)

    def a2a(s, at, rows):
        yrows = pl.ds(al((y * NC + c) * TOK + at, rows), rows)
        xrows = pl.ds(al((x * NC + c) * TOK + at, rows), rows)
        for q_c in range(NC):
            copy_or_send(
                (s == y) & (q_c == c), Xs.at[s, pl.ds(at, rows), pl.ds(q_c * ZW, ZW)], XAy.at[yrows],
                xa_s.at[0], xa_r.at[0], did(s, zh, x, q_c, t),
            )
        q_c = lax.div(s, NS)
        lane = pl.ds(al(lax.rem(s, NS) * NC * L, NC * L), NC * L)

        def one(q, carry):
            src = Xs.at[s, pl.ds(at, rows), pl.ds(al((NX + q) * NC * L, NC * L), NC * L)]
            copy_or_send((q == x) & (q_c == c), src, XAx.at[xrows, lane], xa_s.at[1], xa_r.at[1], did(y, zh, q, q_c, t))
            return carry

        lax.fori_loop(0, NX, one, 0)

    def add_pre(s, at, rows):
        r = pl.ds(at, rows)
        pre[r, :] += jnp.dot(Xs[s, r, :], wgu[pl.ds(al(s * S, S), S), :], preferred_element_type=F32)

    def z_each(k, fn, at=0, rows=TOK):
        @pl.when(t - k - 1 >= 0)
        def _():
            fn(t - k - 1, at, rows)

        @pl.when(t + k + 1 <= NT - 1)
        def _():
            fn(t + k + 1, at, rows)

    def z_pass(k, h):
        z_wait(k, h)
        if k + 1 < NT - 1:
            z_send(k + 1, h)

    HR = H // (NX * NC)
    wrow = pl.ds(al((c * NX + x) * HR, HR), HR)
    crow = pl.ds(al(c * NX * HR, NX * HR), NX * HR)
    orow = pl.ds(al((1 - c) * NX * HR, NX * HR), NX * HR)
    for o in range(1, NT):
        p = lax.rem(t + o, NT)
        send(
            down.at[wrow, pl.ds(al(p * S, S), S)], WdS.at[NT - o, wrow], wd_s.at[0, o - 1], wd_r.at[0, NT - o - 1], (d, p)
        )

    loads[0].wait()
    for o in range(1, NZ):
        q = lax.rem(zh + o, NZ)
        send(RM.at[y, zh, x, c], RM.at[y, zh, x, c], rm_s.at[0], rm_r.at[0, o - 1], did(y, q, x, c, t))

    z_send(0, 0)

    loads[1].wait()
    loads[2].wait()

    def err_rows(i, carry):
        r = pl.ds(al(i * 16, 16), 16)
        err[r, :] = ((stu[r, :].astype(F32) - prj[r, :].astype(F32)) * factor).astype(BF)
        return carry

    lax.fori_loop(0, TOK // 16, err_rows, 0)

    @pl.when(t == 0)
    def _():
        eb[...] = err[:, 0:PB]

    for o in range(1, NT):
        send_if(t == 0, lambda: eb, lambda: eb, eb_s.at[o - 1], eb_r, (d, o))

    for h in range(1, HALVES):
        z_send(0, h)

    LAST = NT - 2

    LAST = NT - 2

    def others(fn):
        for o in range(NX):
            for w in range(NC):
                if o + w > 0:
                    fn(o * NC + w - 1, o, w)

    loads[3].wait()

    loads[5].wait()
    loads[6].wait()
    pre[...] = jnp.dot(Xs[t], wgu[pl.ds(al(t * S, S), S), :], preferred_element_type=F32)

    for o in range(1, NZ):
        arrived(RM.at[y, lax.rem(zh + NZ - o, NZ), x, c], rm_r.at[0, o - 1])
    for o in range(1, NY):
        send(RM.at[y, :, x, c], RM.at[y, :, x, c], rm_s.at[1], rm_r.at[1, o - 1], did(lax.rem(y + o, NY), zh, x, c, t))

    if LAST > 0:
        z_pass(0, 0)

    for o in range(1, NY):
        arrived(RM.at[lax.rem(y + NY - o, NY), :, x, c], rm_r.at[1, o - 1])
    others(lambda i, o, w: send(
        RM.at[:, :, x, c], RM.at[:, :, x, c], rm_s.at[2], rm_r.at[2, i], did(y, zh, lax.rem(x + o, NX), lax.rem(c + w, NC), t)
    ))

    rest = pl.ds(1, NT - 1)
    for o in range(1, NT):
        arrived(WdS.at[o, wrow], wd_r.at[0, o - 1])
    for u in range(1, NX):
        send(WdS.at[rest, wrow], WdS.at[rest, wrow], wd_s.at[1, u - 1], wd_r.at[1, u - 1], did(y, zh, lax.rem(x + u, NX), c, t))

    a2a(t, 0, TOK)

    if LAST > 0:
        z_pass(0, 1)

    others(lambda i, o, w: arrived(RM.at[:, :, lax.rem(x + NX - o, NX), lax.rem(c + NC - w, NC)], rm_r.at[2, i]))

    @pl.when(t != 0)
    def _():
        arrived(eb, eb_r)

    ids = RM[...].reshape(DP, TOK)
    slot = jnp.sum(jnp.where((ids >> shift) == d, ids & (TOK - 1), 0), axis=1, keepdims=True)
    pick = (lax.broadcasted_iota(jnp.int32, (DP, TOK), 1) == slot).astype(F32).astype(BF)
    S0[...] = jnp.dot(pick, eb[...], preferred_element_type=F32).reshape(S0.shape)
    keep = [pltpu.make_async_copy(S0.at[:, :, x, c], S1.at[:, :, x, c], ea_l.at[0])]
    keep[0].start()

    def ea_out(i, o, w):
        q_x, q_c = lax.rem(x + o, NX), lax.rem(c + w, NC)
        send(S0.at[:, :, q_x, q_c], S1.at[:, :, x, c], ea_s.at[0], ea_r.at[0, i], did(y, zh, q_x, q_c, t))

    others(ea_out)

    if LAST > 0:
        z_each(0, a2a)
    if LAST > 1:
        z_pass(1, 0)

    keep[0].wait()
    others(lambda i, o, w: arrived(S1.at[:, :, lax.rem(x + NX - o, NX), lax.rem(c + NC - w, NC)], ea_r.at[0, i]))
    keep.append(pltpu.make_async_copy(S1.at[y], S2.at[y], ea_l.at[1]))
    keep[1].start()
    for o in range(1, NY):
        q = lax.rem(y + o, NY)
        send(S1.at[q], S2.at[y], ea_s.at[1], ea_r.at[1, o - 1], did(q, zh, x, c, t))

    def tea_y(q, carry):
        q_y, q_c = lax.div(q, NC), lax.rem(q, NC)
        src = teacher.at[:, pl.ds(al((q_y * NC + q_c) * NP * ZT, NP * ZT), NP * ZT)]
        copy_or_send((q_y == y) & (q_c == c), src, TAy.at[yrow], ta_s, ta_r, did(q_y, zh, x, q_c, t))
        return carry

    lax.fori_loop(0, NY * NC, tea_y, 0)

    if LAST > 0:
        z_each(0, add_pre)
    if LAST > 1:
        z_pass(1, 1)

    keep[1].wait()
    for o in range(1, NY):
        arrived(S2.at[lax.rem(y + NY - o, NY)], ea_r.at[1, o - 1])
    keep.append(pltpu.make_async_copy(S2.at[:, zh], S3.at[:, zh], ea_l.at[2]))
    keep[2].start()
    for o in range(1, NZ):
        q = lax.rem(zh + o, NZ)
        send(S2.at[:, q], S3.at[:, zh], ea_s.at[2], ea_r.at[2, o - 1], did(y, q, x, c, t))

    if LAST > 1:
        z_each(1, a2a)

    for u in range(1, NX):
        r = pl.ds(al((c * NX + lax.rem(x + NX - u, NX)) * HR, HR), HR)
        arrived(WdS.at[rest, r], wd_r.at[1, u - 1])
    send(WdS.at[rest, crow], WdS.at[rest, crow], wd_s.at[2, 0], wd_r.at[2, 0], did(y, zh, x, 1 - c, t))

    loads[4].wait()
    arrived(WdS.at[rest, orow], wd_r.at[2, 0])
    for k in range(NT):
        actp[k] = lax.dot_general(err[...], WdS[k], (((1,), (1,)), ((), ())), preferred_element_type=F32)
    for k in range(1, NT):
        send(actp.at[k], actr.at[k - 1], act_s.at[k - 1], act_r.at[k - 1], (d, lax.rem(t + k, NT)))

    if LAST > 1:
        z_each(1, add_pre)

    for h in range(HALVES):
        z_pass(LAST, h)
        z_each(LAST, a2a, h * half, half)
        z_each(LAST, add_pre, h * half, half)

    hid, proj_rows = pl.ds(0, 2 * H), pl.ds(2 * H, PB)

    def along_y(rows, ssem, rsem):
        block = GEy.at[rows, yrow]
        for q_c in range(NC):
            for o in range(1, NY):
                send(block, block, ssem, rsem, did(lax.rem(y + o, NY), zh, x, q_c, t))
        send(block, block, ssem, rsem, did(y, zh, x, 1 - c, t))

    def along_x(ssem, rsem):
        block = GEx.at[:, xrow]
        for q_c in range(NC):
            for o in range(1, NX):
                send(block, block, ssem, rsem, did(y, zh, lax.rem(x + o, NX), q_c, t))
        send(block, block, ssem, rsem, did(y, zh, x, 1 - c, t))

    act = actp[0]
    for o in range(1, NT):
        arrived(actr.at[o - 1], act_r.at[o - 1])
        act = act + actr[o - 1]
    gate_pre, up_pre = pre[:, 0:H], pre[:, H : 2 * H]
    sig = jax.nn.sigmoid(gate_pre)
    gate_grad = jnp.transpose(act * up_pre * sig * (1.0 + gate_pre * (1.0 - sig))).astype(BF)
    up_grad = jnp.transpose(act * gate_pre * sig).astype(BF)
    for buf, at in ((GEx, xrow), (GEy, yrow)):
        buf[0:H, at] = gate_grad
        buf[H : 2 * H, at] = up_grad
    along_x(g_s.at[1], g_r.at[1])
    along_y(hid, g_s.at[0], g_r.at[0])

    keep[2].wait()
    for o in range(1, NZ):
        arrived(S3.at[:, lax.rem(zh + NZ - o, NZ)], ea_r.at[2, o - 1])
    order = ((RM[y, zh, x, c] >> shift) == lax.broadcasted_iota(jnp.int32, (DP, 1), 0)).astype(F32).astype(BF)
    GEy[proj_rows, yrow] = lax.dot_general(
        S3[...].reshape(DP, PB).astype(BF), order, (((0,), (0,)), ((), ())), preferred_element_type=F32
    ).astype(BF)

    along_y(proj_rows, e_s, e_r)

    oy, ox = pl.ds(0, (NY * NC - 1) * TOK), pl.ds(0, (NX * NC - 1) * TOK)

    arrived(XAx, xa_r.at[1])
    arrived(GEx.at[:, ox], g_r.at[1])
    tot2 = jnp.dot(GEx[...], XAx[...], preferred_element_type=F32)
    for i in range(NS):
        for q_c in range(NC):
            at = (i * NC + q_c) * L
            msg2[i, q_c, :, 0:L] = tot2[:, at : at + L].astype(BF)
            s = c * NS + i
            copy_or_send(
                (s == y) & (q_c == c), msg2.at[i, q_c], RB2.at[y], r2_s.at[i, q_c], r2_r.at[y], did(s, zh, x, q_c, t)
            )
    arrived(XAy, xa_r.at[0])
    arrived(GEy.at[hid, oy], g_r.at[0])
    tot1 = jnp.dot(GEy[hid, :], XAy[...], preferred_element_type=F32)
    for q in range(NX):
        msg1[q, :, 0:L] = tot1[:, q * L : (q + 1) * L].astype(BF)
        copy_or_send(q == x, msg1.at[q], RB1.at[x], r1_s.at[q], r1_r.at[x], did(y, zh, q, c, t))

    arrived(GEy.at[proj_rows, oy], e_r)
    arrived(TAy, ta_r)
    proj = jnp.transpose(jnp.dot(GEy[proj_rows, :], TAy[...], preferred_element_type=F32)).astype(BF)
    for q in range(NX):
        for j in range(NP):
            at = j * ZT + q * LT
            msgp[q, j * LT : (j + 1) * LT, :] = proj[at : at + LT, :]
        copy_or_send(q == x, msgp.at[q], RBX.at[x], rq_s.at[q], rq_r.at[x], did(y, zh, q, c, t))

    for kind, (buf, sem, count, where) in enumerate(
        ((RB2, r2_r, NY, lambda q_c: (to_z, to_x, q_c)), (RB1, r1_r, NX, lambda q_c: (c, x, q_c)))
    ):
        part = None
        for q in range(count):
            arrived(buf.at[q], sem.at[q])
            part = buf[q].astype(F32) if part is None else part + buf[q].astype(F32)
        feats = jnp.transpose(part[:, 0:L])
        for q_c in range(NC):
            r = slice(q_c * R, (q_c + 1) * R)
            fin[kind, q_c, 0:R, :] = feats[r, 0:H].astype(BF)
            fin[kind, q_c, R : 2 * R, :] = feats[r, H : 2 * H].astype(BF)
            q_z, q_x, _ = where(q_c)
            copy_or_send(
                (q_z == zh) & (q_x == x) & (q_c == c), fin.at[kind, q_c], RB3.at[zh], rb_s.at[kind, q_c], rb_r.at[zh],
                did(y, q_z, q_x, q_c, t),
            )
    part = None
    for q in range(NX):
        arrived(RBX.at[q], rq_r.at[q])
        part = RBX[q].astype(F32) if part is None else part + RBX[q].astype(F32)
    for j in range(NP):
        for q_c in range(NC):
            at = j * LT + q_c * RP
            finp[j, q_c] = part[at : at + RP, :].astype(BF)
            q_z = c * NP + j
            copy_or_send(
                (q_z == zh) & (q_c == c), finp.at[j, q_c], RBP.at[zh], rp_s.at[j, q_c], rp_r.at[zh], did(y, q_z, x, q_c, t)
            )
    result = None
    for q in range(NZ):
        arrived(RB3.at[q], rb_r.at[q])
        result = RB3[q].astype(F32) if result is None else result + RB3[q].astype(F32)
    out[0 : 2 * R, :] = result
    result = None
    for q in range(NZ):
        arrived(RBP.at[q], rp_r.at[q])
        result = RBP[q].astype(F32) if result is None else result + RBP[q].astype(F32)
    out[2 * R : 2 * R + RP, :] = result

    def left(own, ref, sem):
        @pl.when(jnp.logical_not(own))
        def _():
            arrived(ref, sem)

    for copy in drains:
        copy.wait_send()
    for k in range(NT - 1):
        for h in range(HALVES):
            z_drain(k, h)
    for o in range(1, NT):
        left(t != 0, eb, eb_s.at[o - 1])
    for q in range(NX):
        left(q == x, msg1.at[q], r1_s.at[q])
        left(q == x, msgp.at[q], rq_s.at[q])
    for q_c in range(NC):
        for i in range(NS):
            left((c * NS + i == y) & (q_c == c), msg2.at[i, q_c], r2_s.at[i, q_c])
        left((to_z == zh) & (to_x == x) & (q_c == c), fin.at[0, q_c], rb_s.at[0, q_c])
        left((c == zh) & (q_c == c), fin.at[1, q_c], rb_s.at[1, q_c])
        for j in range(NP):
            left((c * NP + j == zh) & (q_c == c), finp.at[j, q_c], rp_s.at[j, q_c])
    arrived(XAy.at[pl.ds(0, (NY * NC - 1) * TOK)], xa_s.at[0])
    arrived(XAx.at[pl.ds(0, (NX * NC - 1) * TOK)], xa_s.at[1])
    arrived(TAy.at[pl.ds(0, (NY * NC - 1) * TOK)], ta_s)


def solution(mesh, pb=128):
    dims = sizes(mesh, pb)
    NY, NX, NT = (dims[k] for k in ("NY", "NX", "NT"))

    def body(teacher_rows, row_map, student_hidden, projected, mlp_input, gate_bucket, up_bucket, down_bucket):
        TOK, S = mlp_input.shape
        F, H = gate_bucket.shape
        DTs = teacher_rows.shape[1]
        NS = NY // NC
        ZW, ZT = S // NZ, DTs // (NY * NZ)
        L, LT = ZW // NX, ZT // NX
        R, RP = L // NC, LT // NC
        NP = NZ // NC
        rows5 = (NY, NZ, NX, NC, 1)
        V, D = pltpu.VMEM, pltpu.SemaphoreType.DMA
        K = NT - 1
        scratch = [
            V((NT, TOK, S), BF), V((TOK, S), BF), V((TOK, S), BF), V((TOK, S), BF),
            V((F, 2 * H), BF), V((NT, H, S), BF),
            V((NY * NC * TOK, NP * ZT), BF),
            V((NY * NC * TOK, ZW), BF), V((NX * NC * TOK, NS * NC * L), BF),
            V((2 * H + pb, NY * NC * TOK), BF), V((2 * H, NX * NC * TOK), BF),
            V((TOK, 2 * H), F32), V((NT, TOK, H), F32), V((K, TOK, H), F32), V((TOK, pb), BF),
            V((*rows5, TOK), jnp.int32), *[V((*rows5, pb), F32)] * 4,
            V((NX, 2 * H, H), BF), V((NS, NC, 2 * H, H), BF), V((NX, NP * LT, pb), BF),
            V((NX, 2 * H, H), BF), V((NY, 2 * H, H), BF), V((NX, NP * LT, pb), BF),
            V((2, NC, 2 * R, H), BF), V((NP, NC, RP, H), BF), V((NZ, 2 * R, H), BF), V((NZ, RP, H), BF),
            D((7,)), D((2, K, HALVES)), D((2, K, HALVES)),
            D((3, 3)), D((3, 3)),
            D((K,)), D,
            D((3,)), D((3, NX * NC)), D((3,)), D((3, NX * NC)), D((3,)),
            D((2,)), D((2,)), D, D,
            D((K,)), D((K,)),
            D, D, D((2,)), D((2,)),
            D((NX,)), D((NX,)), D((NS, NC)), D((NY,)), D((NX,)), D((NX,)), D((2, NC)), D((NZ,)), D((NP, NC)), D((NZ,)),
        ]
        res = pl.pallas_call(
            functools.partial(kernel, dims),
            out_shape=jax.ShapeDtypeStruct((2 * R + RP, H), F32),
            in_specs=[pl.BlockSpec(memory_space=pl.ANY)] * 8,
            out_specs=pl.BlockSpec(memory_space=pltpu.VMEM),
            scratch_shapes=scratch,
            compiler_params=pltpu.CompilerParams(
                collective_id=0, has_side_effects=True, vmem_limit_bytes=VMEM_LIMIT
            ),
        )(teacher_rows, row_map.reshape(1, TOK), student_hidden, projected, mlp_input, gate_bucket, up_bucket, down_bucket)
        return res[2 * R :].T[:, None, :], res[:R].T, res[R : 2 * R].T

    in_specs = (
        P("dp", "tensor"), P("dp"), P("dp", "tensor"), P("dp", "tensor"), P("dp", "tensor"),
        P(None, "tensor"), P(None, "tensor"), P("tensor", None),
    )
    out_specs = (P(None, "tensor", "dp"), P("tensor", "dp"), P("tensor", "dp"))
    return jax.shard_map(body, mesh=mesh, in_specs=in_specs, out_specs=out_specs, check_vma=False)
```

```python
import functools

import jax
import jax.numpy as jnp
from jax import lax
from jax.experimental import pallas as pl
from jax.experimental.pallas import tpu as pltpu
from jax.sharding import PartitionSpec as P

MESH = pl.DeviceIdType.MESH
BF = jnp.bfloat16
F32 = jnp.float32
NC = 2
NZ = 4
HALVES = 2
VMEM_LIMIT = 62 * 1024 * 1024


def sizes(mesh, pb):
    nt = mesh.shape["tensor"]
    return dict(NY=nt, NX=mesh.shape["dp"] // (nt * NZ * NC), NT=nt, PB=pb)


def kernel(
    dims, teacher, rowmap, student, projected, mlp, gate, up, down, out,
    Xs, stu, prj, err, wgu, WdS, TAy, XAy, XAx, GEy, GEx, pre, actp, actr, eb, eb_in,
    RM, S0, S1, S2, S3, S4, msg1, msg2, msgp, RB1, RB2, RBX, fin, finp, RB3, RBP,
    ld, z_s, z_r, wd_s, wd_r, eb_s, eb_r, rm_s, rm_r, ea_s, ea_r, ea_l,
    xa_s, xa_r, ta_s, ta_r, act_s, act_r, e_s, e_r, g_s, g_r, r1_s, r1_r, r2_s, r2_r, rq_s, rq_r, rb_s, rb_r, rp_s, rp_r,
):
    NY, NX, NT, PB = (dims[k] for k in ("NY", "NX", "NT", "PB"))
    NS = NY // NC
    TOK, S = mlp.shape
    H = gate.shape[1]
    DP = NY * NZ * NX * NC
    DTs = teacher.shape[1]
    ZW, ZT = S // NZ, DTs // (NY * NZ)
    L, LT = ZW // NX, ZT // NX
    R, RP = L // NC, LT // NC
    NP = NZ // NC
    d = lax.axis_index("dp")
    t = lax.axis_index("tensor")
    c = lax.rem(d, NC)
    x = lax.rem(lax.div(d, NC), NX)
    zh = lax.rem(lax.div(d, NC * NX), NZ)
    y = lax.div(d, NC * NX * NZ)
    factor = float(TOK * DP) ** -0.5
    shift = TOK.bit_length() - 1
    drains = []

    def did(y_, zh_, x_, c_, t_):
        return (((y_ * NZ + zh_) * NX + x_) * NC + c_, t_)

    def start(src, dst, ssem, rsem, where):
        copy = pltpu.make_async_remote_copy(
            src_ref=src, dst_ref=dst, send_sem=ssem, recv_sem=rsem, device_id=where, device_id_type=MESH
        )
        copy.start()
        return copy

    def send(src, dst, ssem, rsem, where):
        drains.append(start(src, dst, ssem, rsem, where))

    def send_if(cond, src, dst, ssem, rsem, where):
        @pl.when(cond)
        def _():
            start(src(), dst(), ssem, rsem, where)

    def arrived(ref, sem):
        pltpu.make_async_copy(ref, ref, sem).wait()

    def copy_or_send(own, src, dst, ssem, rsem, where):
        @pl.when(own)
        def _():
            pltpu.make_async_copy(src, dst, rsem).start()

        @pl.when(jnp.logical_not(own))
        def _():
            start(src, dst, ssem, rsem, where)

    def al(v, m):
        return pl.multiple_of(v, m)

    half = TOK // HALVES

    def rows_of(h):
        return pl.ds(h * half, half)

    loads = [
        pltpu.make_async_copy(rowmap, RM.at[y, zh, x, c], ld.at[0]),
        pltpu.make_async_copy(student, stu, ld.at[1]),
        pltpu.make_async_copy(projected, prj, ld.at[2]),
        pltpu.make_async_copy(mlp, Xs.at[t], ld.at[3]),
        pltpu.make_async_copy(down.at[:, pl.ds(al(t * S, S), S)], WdS.at[0], ld.at[4]),
        pltpu.make_async_copy(gate, wgu.at[:, pl.ds(0, H)], ld.at[5]),
        pltpu.make_async_copy(up, wgu.at[:, pl.ds(H, H)], ld.at[6]),
        pltpu.make_async_copy(student.at[:, pl.ds(0, PB)], eb_in.at[0], ld.at[7]),
        pltpu.make_async_copy(projected.at[:, pl.ds(0, PB)], eb_in.at[1], ld.at[8]),
    ]
    for copy in loads[7:] + loads[:7]:
        copy.start()

    to_z = NC + lax.div(x * NC, NX)
    to_x = lax.rem(x * NC, NX) + c
    blk = (zh - NC) * NX + x
    from_x = jnp.where(zh < NC, x, lax.div(blk, NC))
    from_c = jnp.where(zh < NC, zh, lax.rem(blk, NC))

    barrier = pltpu.get_barrier_semaphore()

    def greet(where):
        pl.semaphore_signal(barrier, inc=1, device_id=where, device_id_type=MESH)

    for q_c in range(NC):
        for o in range(1, NX):
            greet(did(y, zh, lax.rem(x + o, NX), q_c, t))
        for o in range(1, NY):
            greet(did(lax.rem(y + o, NY), zh, x, q_c, t))
    greet(did(y, zh, x, 1 - c, t))
    for o in range(1, NZ):
        greet(did(y, lax.rem(zh + o, NZ), x, c, t))
    for o in range(1, NT):
        greet((d, lax.rem(t + o, NT)))
    for q in range(NZ):
        @pl.when(jnp.logical_not((q == zh) & (from_x == x) & (from_c == c)))
        def _():
            greet(did(y, q, from_x, from_c, t))
        @pl.when(jnp.logical_not((q == zh) & (lax.div(zh, NP) == c)))
        def _():
            greet(did(y, q, x, lax.div(zh, NP), t))
    loads[7].wait()
    loads[8].wait()

    @pl.when(t == 0)
    def _():
        eb[...] = ((eb_in[0].astype(F32) - eb_in[1].astype(F32)) * factor).astype(BF)

    to_self = (c == zh) | ((to_z == zh) & (to_x == x))
    to_self_p = lax.div(zh, NP) == c
    pl.semaphore_wait(
        barrier,
        (NX - 1 + NY - 1) * NC + 1 + NZ - 1 + NT - 1 + 2 * NC + NP * NC
        - jnp.where(to_self, 1, 0) - jnp.where(to_self_p, 1, 0),
    )

    def z_send(k, h):
        sr, sl = t - k, t + k
        rows = rows_of(h)
        src_r = (lambda: mlp.at[rows]) if k == 0 else (lambda: Xs.at[sr, rows])
        src_l = (lambda: mlp.at[rows]) if k == 0 else (lambda: Xs.at[sl, rows])
        send_if((sr >= 0) & (t < NT - 1), src_r, lambda: Xs.at[sr, rows], z_s.at[0, k, h], z_r.at[0, k, h], (d, t + 1))
        send_if((sl <= NT - 1) & (t > 0), src_l, lambda: Xs.at[sl, rows], z_s.at[1, k, h], z_r.at[1, k, h], (d, t - 1))

    def z_drain(k, h):
        sr, sl = t - k, t + k

        @pl.when((sr >= 0) & (t < NT - 1))
        def _():
            arrived(Xs.at[sr, rows_of(h)], z_s.at[0, k, h])

        @pl.when((sl <= NT - 1) & (t > 0))
        def _():
            arrived(Xs.at[sl, rows_of(h)], z_s.at[1, k, h])

    def z_wait(k, h):
        @pl.when(t - k - 1 >= 0)
        def _():
            arrived(Xs.at[t - k - 1, rows_of(h)], z_r.at[0, k, h])

        @pl.when(t + k + 1 <= NT - 1)
        def _():
            arrived(Xs.at[t + k + 1, rows_of(h)], z_r.at[1, k, h])

    yrow = pl.ds(al((y * NC + c) * TOK, TOK), TOK)
    xrow = pl.ds(al((x * NC + c) * TOK, TOK), TOK)

    def a2a(s, at, rows):
        yrows = pl.ds(al((y * NC + c) * TOK + at, rows), rows)
        xrows = pl.ds(al((x * NC + c) * TOK + at, rows), rows)
        for q_c in range(NC):
            copy_or_send(
                (s == y) & (q_c == c), Xs.at[s, pl.ds(at, rows), pl.ds(q_c * ZW, ZW)], XAy.at[yrows],
                xa_s.at[0], xa_r.at[0], did(s, zh, x, q_c, t),
            )
        q_c = lax.div(s, NS)
        lane = pl.ds(al(lax.rem(s, NS) * NC * L, NC * L), NC * L)

        def one(q, carry):
            src = Xs.at[s, pl.ds(at, rows), pl.ds(al((NX + q) * NC * L, NC * L), NC * L)]
            copy_or_send((q == x) & (q_c == c), src, XAx.at[xrows, lane], xa_s.at[1], xa_r.at[1], did(y, zh, q, q_c, t))
            return carry

        lax.fori_loop(0, NX, one, 0)

    def add_pre(s, at, rows):
        r = pl.ds(at, rows)
        pre[r, :] += jnp.dot(Xs[s, r, :], wgu[pl.ds(al(s * S, S), S), :], preferred_element_type=F32)

    def z_each(k, fn, at=0, rows=TOK):
        @pl.when(t - k - 1 >= 0)
        def _():
            fn(t - k - 1, at, rows)

        @pl.when(t + k + 1 <= NT - 1)
        def _():
            fn(t + k + 1, at, rows)

    def z_pass(k, h):
        z_wait(k, h)
        if k + 1 < NT - 1:
            z_send(k + 1, h)

    loads[0].wait()
    for o in range(1, NZ):
        q = lax.rem(zh + o, NZ)
        send(RM.at[y, zh, x, c], RM.at[y, zh, x, c], rm_s.at[0], rm_r.at[0, o - 1], did(y, q, x, c, t))

    for o in range(1, NT):
        send_if(t == 0, lambda: eb, lambda: eb, eb_s.at[o - 1], eb_r, (d, o))

    HR, SQ = H // (NX * NC), S // NY
    ycols = pl.ds(al(y * SQ, SQ), SQ)
    wrow = pl.ds(al((c * NX + x) * HR, HR), HR)
    crow = pl.ds(al(c * NX * HR, NX * HR), NX * HR)
    orow = pl.ds(al((1 - c) * NX * HR, NX * HR), NX * HR)
    for o in range(1, NT):
        p = lax.rem(t + o, NT)
        send(
            down.at[wrow, pl.ds(al(p * S + y * SQ, SQ), SQ)], WdS.at[NT - o, wrow, ycols], wd_s.at[0, o - 1], wd_r.at[0, NT - o - 1], (d, p)
        )

    for h in range(HALVES):
        z_send(0, h)

    loads[1].wait()
    loads[2].wait()

    def err_rows(i, carry):
        r = pl.ds(al(i * 16, 16), 16)
        err[r, :] = ((stu[r, :].astype(F32) - prj[r, :].astype(F32)) * factor).astype(BF)
        return carry

    lax.fori_loop(0, TOK // 16, err_rows, 0)

    LAST = NT - 2

    def others(fn):
        for o in range(NX):
            for w in range(NC):
                if o + w > 0:
                    fn(o * NC + w - 1, o, w)

    loads[3].wait()

    loads[5].wait()
    loads[6].wait()
    pre[...] = jnp.dot(Xs[t], wgu[pl.ds(al(t * S, S), S), :], preferred_element_type=F32)

    for o in range(1, NZ):
        arrived(RM.at[y, lax.rem(zh + NZ - o, NZ), x, c], rm_r.at[0, o - 1])
    for o in range(1, NY):
        send(RM.at[y, :, x, c], RM.at[y, :, x, c], rm_s.at[1], rm_r.at[1, o - 1], did(lax.rem(y + o, NY), zh, x, c, t))

    rest = pl.ds(1, NT - 1)
    for o in range(1, NT):
        arrived(WdS.at[o, wrow, ycols], wd_r.at[0, o - 1])
    for u in range(1, NY):
        send(
            WdS.at[rest, wrow, ycols], WdS.at[rest, wrow, ycols], wd_s.at[3, u - 1], wd_r.at[3, u - 1],
            did(lax.rem(y + u, NY), zh, x, c, t),
        )

    def tea_y(q, carry):
        q_y, q_c = lax.div(q, NC), lax.rem(q, NC)
        src = teacher.at[:, pl.ds(al((q_y * NC + q_c) * NP * ZT, NP * ZT), NP * ZT)]
        copy_or_send((q_y == y) & (q_c == c), src, TAy.at[yrow], ta_s, ta_r, did(q_y, zh, x, q_c, t))
        return carry

    lax.fori_loop(0, NY * NC, tea_y, 0)

    if LAST > 0:
        z_pass(0, 0)

    for o in range(1, NY):
        arrived(RM.at[lax.rem(y + NY - o, NY), :, x, c], rm_r.at[1, o - 1])
    others(lambda i, o, w: send(
        RM.at[:, :, x, c], RM.at[:, :, x, c], rm_s.at[2], rm_r.at[2, i], did(y, zh, lax.rem(x + o, NX), lax.rem(c + w, NC), t)
    ))

    for u in range(1, NY):
        cols = pl.ds(al(lax.rem(y + NY - u, NY) * SQ, SQ), SQ)
        arrived(WdS.at[rest, wrow, cols], wd_r.at[3, u - 1])
    for u in range(1, NX):
        send(WdS.at[rest, wrow], WdS.at[rest, wrow], wd_s.at[1, u - 1], wd_r.at[1, u - 1], did(y, zh, lax.rem(x + u, NX), c, t))

    a2a(t, 0, TOK)

    if LAST > 0:
        z_pass(0, 1)

    others(lambda i, o, w: arrived(RM.at[:, :, lax.rem(x + NX - o, NX), lax.rem(c + NC - w, NC)], rm_r.at[2, i]))

    @pl.when(t != 0)
    def _():
        arrived(eb, eb_r)

    ids = RM[...].reshape(DP, TOK)
    slot = jnp.sum(jnp.where((ids >> shift) == d, ids & (TOK - 1), 0), axis=1, keepdims=True)
    pick = (lax.broadcasted_iota(jnp.int32, (DP, TOK), 1) == slot).astype(F32).astype(BF)
    S0[...] = jnp.dot(pick, eb[...], preferred_element_type=F32).reshape(S0.shape)
    keep = [pltpu.make_async_copy(S0.at[:, :, x, c], S1.at[:, :, x, c], ea_l.at[0])]
    keep[0].start()

    def ea_out(i, o, w):
        q_x, q_c = lax.rem(x + o, NX), lax.rem(c + w, NC)
        send(S0.at[:, :, q_x, q_c], S1.at[:, :, x, c], ea_s.at[0], ea_r.at[0, i], did(y, zh, q_x, q_c, t))

    others(ea_out)

    if LAST > 0:
        z_each(0, a2a)
    if LAST > 1:
        z_pass(1, 0)

    keep[0].wait()
    others(lambda i, o, w: arrived(S1.at[:, :, lax.rem(x + NX - o, NX), lax.rem(c + NC - w, NC)], ea_r.at[0, i]))
    keep.append(pltpu.make_async_copy(S1.at[y], S2.at[y], ea_l.at[1]))
    keep[1].start()
    for o in range(1, NY):
        q = lax.rem(y + o, NY)
        send(S1.at[q], S2.at[y], ea_s.at[1], ea_r.at[1, o - 1], did(q, zh, x, c, t))

    if LAST > 1:
        z_pass(1, 1)

    if LAST > 1:
        z_each(1, a2a)

    keep[1].wait()
    for o in range(1, NY):
        arrived(S2.at[lax.rem(y + NY - o, NY)], ea_r.at[1, o - 1])
    for q in range(NZ):
        S3[q] = S2[:, q].reshape(DP // NZ, PB).astype(BF)
    for o in range(1, NZ):
        q = lax.rem(zh + o, NZ)
        send(S3.at[q], S4.at[zh], ea_s.at[2], ea_r.at[2, o - 1], did(y, q, x, c, t))
    S4[zh] = S3[zh]

    if LAST > 0:
        z_each(0, add_pre)
    for u in range(1, NX):
        r = pl.ds(al((c * NX + lax.rem(x + NX - u, NX)) * HR, HR), HR)
        arrived(WdS.at[rest, r], wd_r.at[1, u - 1])
    send(WdS.at[rest, crow], WdS.at[rest, crow], wd_s.at[2, 0], wd_r.at[2, 0], did(y, zh, x, 1 - c, t))

    loads[4].wait()
    arrived(WdS.at[rest, orow], wd_r.at[2, 0])
    for k in range(NT):
        actp[k] = lax.dot_general(err[...], WdS[k], (((1,), (1,)), ((), ())), preferred_element_type=F32)
    for k in range(1, NT):
        send(actp.at[k], actr.at[k - 1], act_s.at[k - 1], act_r.at[k - 1], (d, lax.rem(t + k, NT)))

    if LAST > 1:
        z_each(1, add_pre)

    hid, proj_rows = pl.ds(0, 2 * H), pl.ds(2 * H, PB)

    def along_y(rows, ssem, rsem):
        block = GEy.at[rows, yrow]
        for q_c in range(NC):
            for o in range(1, NY):
                send(block, block, ssem, rsem, did(lax.rem(y + o, NY), zh, x, q_c, t))
        send(block, block, ssem, rsem, did(y, zh, x, 1 - c, t))

    def along_x(ssem, rsem):
        block = GEx.at[:, xrow]
        for q_c in range(NC):
            for o in range(1, NX):
                send(block, block, ssem, rsem, did(y, zh, lax.rem(x + o, NX), q_c, t))
        send(block, block, ssem, rsem, did(y, zh, x, 1 - c, t))

    def z_last(h):
        z_pass(LAST, h)
        z_each(LAST, a2a, h * half, half)
        z_each(LAST, add_pre, h * half, half)

    z_last(0)

    for o in range(1, NZ):
        arrived(S4.at[lax.rem(zh + NZ - o, NZ)], ea_r.at[2, o - 1])
    row = lax.broadcasted_iota(jnp.int32, (DP, 1), 0)
    group, place = lax.div(row, DP // NZ), lax.rem(row, DP // NZ)
    row_d = (lax.div(place, NX * NC) * NZ + group) * (NX * NC) + lax.rem(place, NX * NC)
    order = ((RM[y, zh, x, c] >> shift) == row_d).astype(F32).astype(BF)
    GEy[proj_rows, yrow] = lax.dot_general(
        S4[...].reshape(DP, PB), order, (((0,), (0,)), ((), ())), preferred_element_type=F32
    ).astype(BF)

    along_y(proj_rows, e_s, e_r)

    for h in range(1, HALVES):
        z_last(h)

    act = actp[0]
    for o in range(1, NT):
        arrived(actr.at[o - 1], act_r.at[o - 1])
        act = act + actr[o - 1]
    gate_pre, up_pre = pre[:, 0:H], pre[:, H : 2 * H]
    sig = jax.nn.sigmoid(gate_pre)
    gate_grad = jnp.transpose(act * up_pre * sig * (1.0 + gate_pre * (1.0 - sig))).astype(BF)
    up_grad = jnp.transpose(act * gate_pre * sig).astype(BF)
    for buf, at in ((GEx, xrow), (GEy, yrow)):
        buf[0:H, at] = gate_grad
        buf[H : 2 * H, at] = up_grad
    along_x(g_s.at[1], g_r.at[1])
    along_y(hid, g_s.at[0], g_r.at[0])

    oy, ox = pl.ds(0, (NY * NC - 1) * TOK), pl.ds(0, (NX * NC - 1) * TOK)

    arrived(GEy.at[proj_rows, oy], e_r)
    arrived(TAy, ta_r)
    proj = jnp.transpose(jnp.dot(GEy[proj_rows, :], TAy[...], preferred_element_type=F32)).astype(BF)
    for q in range(NX):
        for j in range(NP):
            at = j * ZT + q * LT
            msgp[q, j * LT : (j + 1) * LT, :] = proj[at : at + LT, :]
        copy_or_send(q == x, msgp.at[q], RBX.at[x], rq_s.at[q], rq_r.at[x], did(y, zh, q, c, t))

    arrived(XAx, xa_r.at[1])
    arrived(GEx.at[:, ox], g_r.at[1])
    tot2 = jnp.dot(GEx[...], XAx[...], preferred_element_type=F32)
    for i in range(NS):
        for q_c in range(NC):
            at = (i * NC + q_c) * L
            msg2[i, q_c, :, 0:L] = tot2[:, at : at + L].astype(BF)
            s = c * NS + i
            copy_or_send(
                (s == y) & (q_c == c), msg2.at[i, q_c], RB2.at[y], r2_s.at[i, q_c], r2_r.at[y], did(s, zh, x, q_c, t)
            )
    arrived(XAy, xa_r.at[0])
    arrived(GEy.at[hid, oy], g_r.at[0])
    tot1 = jnp.dot(GEy[hid, :], XAy[...], preferred_element_type=F32)
    for q in range(NX):
        msg1[q, :, 0:L] = tot1[:, q * L : (q + 1) * L].astype(BF)
        copy_or_send(q == x, msg1.at[q], RB1.at[x], r1_s.at[q], r1_r.at[x], did(y, zh, q, c, t))

    part = None
    for q in range(NX):
        arrived(RBX.at[q], rq_r.at[q])
        part = RBX[q].astype(F32) if part is None else part + RBX[q].astype(F32)
    for j in range(NP):
        for q_c in range(NC):
            at = j * LT + q_c * RP
            finp[j, q_c] = part[at : at + RP, :].astype(BF)
            q_z = c * NP + j
            copy_or_send(
                (q_z == zh) & (q_c == c), finp.at[j, q_c], RBP.at[zh], rp_s.at[j, q_c], rp_r.at[zh], did(y, q_z, x, q_c, t)
            )
    for kind, (buf, sem, count, where) in enumerate(
        ((RB2, r2_r, NY, lambda q_c: (to_z, to_x, q_c)), (RB1, r1_r, NX, lambda q_c: (c, x, q_c)))
    ):
        part = None
        for q in range(count):
            arrived(buf.at[q], sem.at[q])
            part = buf[q].astype(F32) if part is None else part + buf[q].astype(F32)
        feats = jnp.transpose(part[:, 0:L])
        for q_c in range(NC):
            r = slice(q_c * R, (q_c + 1) * R)
            fin[kind, q_c, 0:R, :] = feats[r, 0:H].astype(BF)
            fin[kind, q_c, R : 2 * R, :] = feats[r, H : 2 * H].astype(BF)
            q_z, q_x, _ = where(q_c)
            copy_or_send(
                (q_z == zh) & (q_x == x) & (q_c == c), fin.at[kind, q_c], RB3.at[zh], rb_s.at[kind, q_c], rb_r.at[zh],
                did(y, q_z, q_x, q_c, t),
            )
    result = None
    for q in range(NZ):
        arrived(RB3.at[q], rb_r.at[q])
        result = RB3[q].astype(F32) if result is None else result + RB3[q].astype(F32)
    out[0 : 2 * R, :] = result
    result = None
    for q in range(NZ):
        arrived(RBP.at[q], rp_r.at[q])
        result = RBP[q].astype(F32) if result is None else result + RBP[q].astype(F32)
    out[2 * R : 2 * R + RP, :] = result

    def left(own, ref, sem):
        @pl.when(jnp.logical_not(own))
        def _():
            arrived(ref, sem)

    for copy in drains:
        copy.wait_send()
    for k in range(NT - 1):
        for h in range(HALVES):
            z_drain(k, h)
    for o in range(1, NT):
        left(t != 0, eb, eb_s.at[o - 1])
    for q in range(NX):
        left(q == x, msg1.at[q], r1_s.at[q])
        left(q == x, msgp.at[q], rq_s.at[q])
    for q_c in range(NC):
        for i in range(NS):
            left((c * NS + i == y) & (q_c == c), msg2.at[i, q_c], r2_s.at[i, q_c])
        left((to_z == zh) & (to_x == x) & (q_c == c), fin.at[0, q_c], rb_s.at[0, q_c])
        left((c == zh) & (q_c == c), fin.at[1, q_c], rb_s.at[1, q_c])
        for j in range(NP):
            left((c * NP + j == zh) & (q_c == c), finp.at[j, q_c], rp_s.at[j, q_c])
    arrived(XAy.at[pl.ds(0, (NY * NC - 1) * TOK)], xa_s.at[0])
    arrived(XAx.at[pl.ds(0, (NX * NC - 1) * TOK)], xa_s.at[1])
    arrived(TAy.at[pl.ds(0, (NY * NC - 1) * TOK)], ta_s)


def solution(mesh, pb=128):
    dims = sizes(mesh, pb)
    NY, NX, NT = (dims[k] for k in ("NY", "NX", "NT"))

    def body(teacher_rows, row_map, student_hidden, projected, mlp_input, gate_bucket, up_bucket, down_bucket):
        TOK, S = mlp_input.shape
        F, H = gate_bucket.shape
        DTs = teacher_rows.shape[1]
        NS = NY // NC
        ZW, ZT = S // NZ, DTs // (NY * NZ)
        L, LT = ZW // NX, ZT // NX
        R, RP = L // NC, LT // NC
        NP = NZ // NC
        rows5 = (NY, NZ, NX, NC, 1)
        V, D = pltpu.VMEM, pltpu.SemaphoreType.DMA
        K = NT - 1
        scratch = [
            V((NT, TOK, S), BF), V((TOK, S), BF), V((TOK, S), BF), V((TOK, S), BF),
            V((F, 2 * H), BF), V((NT, H, S), BF),
            V((NY * NC * TOK, NP * ZT), BF),
            V((NY * NC * TOK, ZW), BF), V((NX * NC * TOK, NS * NC * L), BF),
            V((2 * H + pb, NY * NC * TOK), BF), V((2 * H, NX * NC * TOK), BF),
            V((TOK, 2 * H), F32), V((NT, TOK, H), F32), V((K, TOK, H), F32), V((TOK, pb), BF), V((2, TOK, pb), BF),
            V((*rows5, TOK), jnp.int32), *[V((*rows5, pb), F32)] * 3,
            *[V((NZ, NY * NX * NC, pb), BF)] * 2,
            V((NX, 2 * H, H), BF), V((NS, NC, 2 * H, H), BF), V((NX, NP * LT, pb), BF),
            V((NX, 2 * H, H), BF), V((NY, 2 * H, H), BF), V((NX, NP * LT, pb), BF),
            V((2, NC, 2 * R, H), BF), V((NP, NC, RP, H), BF), V((NZ, 2 * R, H), BF), V((NZ, RP, H), BF),
            D((9,)), D((2, K, HALVES)), D((2, K, HALVES)),
            D((4, 3)), D((4, 3)),
            D((K,)), D,
            D((3,)), D((3, NX * NC)), D((3,)), D((3, NX * NC)), D((3,)),
            D((2,)), D((2,)), D, D,
            D((K,)), D((K,)),
            D, D, D((2,)), D((2,)),
            D((NX,)), D((NX,)), D((NS, NC)), D((NY,)), D((NX,)), D((NX,)), D((2, NC)), D((NZ,)), D((NP, NC)), D((NZ,)),
        ]
        res = pl.pallas_call(
            functools.partial(kernel, dims),
            out_shape=jax.ShapeDtypeStruct((2 * R + RP, H), F32),
            in_specs=[pl.BlockSpec(memory_space=pl.ANY)] * 8,
            out_specs=pl.BlockSpec(memory_space=pltpu.VMEM),
            scratch_shapes=scratch,
            compiler_params=pltpu.CompilerParams(
                collective_id=0, has_side_effects=True, vmem_limit_bytes=VMEM_LIMIT
            ),
        )(teacher_rows, row_map.reshape(1, TOK), student_hidden, projected, mlp_input, gate_bucket, up_bucket, down_bucket)
        return res[2 * R :].T[:, None, :], res[:R].T, res[R : 2 * R].T

    in_specs = (
        P("dp", "tensor"), P("dp"), P("dp", "tensor"), P("dp", "tensor"), P("dp", "tensor"),
        P(None, "tensor"), P(None, "tensor"), P("tensor", None),
    )
    out_specs = (P(None, "tensor", "dp"), P("tensor", "dp"), P("tensor", "dp"))
    return jax.shard_map(body, mesh=mesh, in_specs=in_specs, out_specs=out_specs, check_vma=False)
```

```python
import functools

import jax
import jax.numpy as jnp
from jax import lax
from jax.experimental import pallas as pl
from jax.experimental.pallas import tpu as pltpu
from jax.sharding import PartitionSpec as P

MESH = pl.DeviceIdType.MESH
BF = jnp.bfloat16
F32 = jnp.float32
NC = 2
NZ = 4
HALVES = 2
VMEM_LIMIT = 62 * 1024 * 1024


def sizes(mesh, pb):
    nt = mesh.shape["tensor"]
    return dict(NY=nt, NX=mesh.shape["dp"] // (nt * NZ * NC), NT=nt, PB=pb)


def kernel(
    dims, teacher, rowmap, student, projected, mlp, gate, up, down, out,
    Xs, stu, prj, err, wgu, WdS, TAy, XAy, XAx, GEy, GEx, pre, actp, actr, eb, eb_in,
    RM, S0, S1, S2, S3, S4, msg1, msg2, msgp, RB1, RB2, RBX, fin, finp, RB3, RBP,
    ld, z_s, z_r, wd_s, wd_r, eb_s, eb_r, rm_s, rm_r, ea_s, ea_r, ea_l,
    xa_s, xa_r, ta_s, ta_r, act_s, act_r, e_s, e_r, g_s, g_r, r1_s, r1_r, r2_s, r2_r, rq_s, rq_r, rb_s, rb_r, rp_s, rp_r,
):
    NY, NX, NT, PB = (dims[k] for k in ("NY", "NX", "NT", "PB"))
    NS = NY // NC
    TOK, S = mlp.shape
    H = gate.shape[1]
    DP = NY * NZ * NX * NC
    DTs = teacher.shape[1]
    ZW, ZT = S // NZ, DTs // (NY * NZ)
    L, LT = ZW // NX, ZT // NX
    R, RP = L // NC, LT // NC
    NP = NZ // NC
    d = lax.axis_index("dp")
    t = lax.axis_index("tensor")
    c = lax.rem(d, NC)
    x = lax.rem(lax.div(d, NC), NX)
    zh = lax.rem(lax.div(d, NC * NX), NZ)
    y = lax.div(d, NC * NX * NZ)
    factor = float(TOK * DP) ** -0.5
    shift = TOK.bit_length() - 1
    drains = []

    def did(y_, zh_, x_, c_, t_):
        return (((y_ * NZ + zh_) * NX + x_) * NC + c_, t_)

    def start(src, dst, ssem, rsem, where):
        copy = pltpu.make_async_remote_copy(
            src_ref=src, dst_ref=dst, send_sem=ssem, recv_sem=rsem, device_id=where, device_id_type=MESH
        )
        copy.start()
        return copy

    def send(src, dst, ssem, rsem, where):
        drains.append(start(src, dst, ssem, rsem, where))

    def send_if(cond, src, dst, ssem, rsem, where):
        @pl.when(cond)
        def _():
            start(src(), dst(), ssem, rsem, where)

    def arrived(ref, sem):
        pltpu.make_async_copy(ref, ref, sem).wait()

    def copy_or_send(own, src, dst, ssem, rsem, where):
        @pl.when(own)
        def _():
            pltpu.make_async_copy(src, dst, rsem).start()

        @pl.when(jnp.logical_not(own))
        def _():
            start(src, dst, ssem, rsem, where)

    def al(v, m):
        return pl.multiple_of(v, m)

    half = TOK // HALVES

    def rows_of(h):
        return pl.ds(h * half, half)

    loads = [
        pltpu.make_async_copy(rowmap, RM.at[y, zh, x, c], ld.at[0]),
        pltpu.make_async_copy(student, stu, ld.at[1]),
        pltpu.make_async_copy(projected, prj, ld.at[2]),
        pltpu.make_async_copy(mlp, Xs.at[t], ld.at[3]),
        pltpu.make_async_copy(down.at[:, pl.ds(al(t * S, S), S)], WdS.at[0], ld.at[4]),
        pltpu.make_async_copy(gate, wgu.at[:, pl.ds(0, H)], ld.at[5]),
        pltpu.make_async_copy(up, wgu.at[:, pl.ds(H, H)], ld.at[6]),
        pltpu.make_async_copy(student.at[:, pl.ds(0, PB)], eb_in.at[0], ld.at[7]),
        pltpu.make_async_copy(projected.at[:, pl.ds(0, PB)], eb_in.at[1], ld.at[8]),
    ]
    for copy in loads[7:] + loads[:7]:
        copy.start()

    to_z = NC + lax.div(x * NC, NX)
    to_x = lax.rem(x * NC, NX) + c
    blk = (zh - NC) * NX + x
    from_x = jnp.where(zh < NC, x, lax.div(blk, NC))
    from_c = jnp.where(zh < NC, zh, lax.rem(blk, NC))

    barrier = pltpu.get_barrier_semaphore()

    def greet(where):
        pl.semaphore_signal(barrier, inc=1, device_id=where, device_id_type=MESH)

    for q_c in range(NC):
        for o in range(1, NX):
            greet(did(y, zh, lax.rem(x + o, NX), q_c, t))
        for o in range(1, NY):
            greet(did(lax.rem(y + o, NY), zh, x, q_c, t))
    greet(did(y, zh, x, 1 - c, t))
    for o in range(1, NZ):
        greet(did(y, lax.rem(zh + o, NZ), x, c, t))
    for o in range(1, NT):
        greet((d, lax.rem(t + o, NT)))
    for q in range(NZ):
        @pl.when(jnp.logical_not((q == zh) & (from_x == x) & (from_c == c)))
        def _():
            greet(did(y, q, from_x, from_c, t))
        @pl.when(jnp.logical_not((q == zh) & (lax.div(zh, NP) == c)))
        def _():
            greet(did(y, q, x, lax.div(zh, NP), t))
    loads[7].wait()
    loads[8].wait()

    @pl.when(t == 0)
    def _():
        eb[...] = ((eb_in[0].astype(F32) - eb_in[1].astype(F32)) * factor).astype(BF)

    to_self = (c == zh) | ((to_z == zh) & (to_x == x))
    to_self_p = lax.div(zh, NP) == c
    pl.semaphore_wait(
        barrier,
        (NX - 1 + NY - 1) * NC + 1 + NZ - 1 + NT - 1 + 2 * NC + NP * NC
        - jnp.where(to_self, 1, 0) - jnp.where(to_self_p, 1, 0),
    )

    def z_send(k, h):
        sr, sl = t - k, t + k
        rows = rows_of(h)
        src_r = (lambda: mlp.at[rows]) if k == 0 else (lambda: Xs.at[sr, rows])
        src_l = (lambda: mlp.at[rows]) if k == 0 else (lambda: Xs.at[sl, rows])
        send_if((sr >= 0) & (t < NT - 1), src_r, lambda: Xs.at[sr, rows], z_s.at[0, k, h], z_r.at[0, k, h], (d, t + 1))
        send_if((sl <= NT - 1) & (t > 0), src_l, lambda: Xs.at[sl, rows], z_s.at[1, k, h], z_r.at[1, k, h], (d, t - 1))

    def z_drain(k, h):
        sr, sl = t - k, t + k

        @pl.when((sr >= 0) & (t < NT - 1))
        def _():
            arrived(Xs.at[sr, rows_of(h)], z_s.at[0, k, h])

        @pl.when((sl <= NT - 1) & (t > 0))
        def _():
            arrived(Xs.at[sl, rows_of(h)], z_s.at[1, k, h])

    def z_wait(k, h):
        @pl.when(t - k - 1 >= 0)
        def _():
            arrived(Xs.at[t - k - 1, rows_of(h)], z_r.at[0, k, h])

        @pl.when(t + k + 1 <= NT - 1)
        def _():
            arrived(Xs.at[t + k + 1, rows_of(h)], z_r.at[1, k, h])

    yrow = pl.ds(al((y * NC + c) * TOK, TOK), TOK)
    xrow = pl.ds(al((x * NC + c) * TOK, TOK), TOK)

    def a2a(s, at, rows):
        yrows = pl.ds(al((y * NC + c) * TOK + at, rows), rows)
        xrows = pl.ds(al((x * NC + c) * TOK + at, rows), rows)
        for q_c in range(NC):
            copy_or_send(
                (s == y) & (q_c == c), Xs.at[s, pl.ds(at, rows), pl.ds(q_c * ZW, ZW)], XAy.at[yrows],
                xa_s.at[0], xa_r.at[0], did(s, zh, x, q_c, t),
            )
        q_c = lax.div(s, NS)
        lane = pl.ds(al(lax.rem(s, NS) * NC * L, NC * L), NC * L)

        def one(q, carry):
            src = Xs.at[s, pl.ds(at, rows), pl.ds(al((NX + q) * NC * L, NC * L), NC * L)]
            copy_or_send((q == x) & (q_c == c), src, XAx.at[xrows, lane], xa_s.at[1], xa_r.at[1], did(y, zh, q, q_c, t))
            return carry

        lax.fori_loop(0, NX, one, 0)

    def add_pre(s, at, rows):
        r = pl.ds(at, rows)
        pre[r, :] += jnp.dot(Xs[s, r, :], wgu[pl.ds(al(s * S, S), S), :], preferred_element_type=F32)

    def z_each(k, fn, at=0, rows=TOK):
        @pl.when(t - k - 1 >= 0)
        def _():
            fn(t - k - 1, at, rows)

        @pl.when(t + k + 1 <= NT - 1)
        def _():
            fn(t + k + 1, at, rows)

    def z_pass(k, h):
        z_wait(k, h)
        if k + 1 < NT - 1:
            z_send(k + 1, h)

    loads[0].wait()
    for o in range(1, NZ):
        q = lax.rem(zh + o, NZ)
        send(RM.at[y, zh, x, c], RM.at[y, zh, x, c], rm_s.at[0], rm_r.at[0, o - 1], did(y, q, x, c, t))

    for o in range(1, NT):
        send_if(t == 0, lambda: eb, lambda: eb, eb_s.at[o - 1], eb_r, (d, o))

    HR, SQ = H // (NX * NC), S // NY
    ycols = pl.ds(al(y * SQ, SQ), SQ)
    wrow = pl.ds(al((c * NX + x) * HR, HR), HR)
    crow = pl.ds(al(c * NX * HR, NX * HR), NX * HR)
    orow = pl.ds(al((1 - c) * NX * HR, NX * HR), NX * HR)
    for o in range(1, NT):
        p = lax.rem(t + o, NT)
        send(
            down.at[wrow, pl.ds(al(p * S + y * SQ, SQ), SQ)], WdS.at[NT - o, wrow, ycols], wd_s.at[0, o - 1], wd_r.at[0, NT - o - 1], (d, p)
        )

    for h in range(HALVES):
        z_send(0, h)

    loads[1].wait()
    loads[2].wait()

    def err_rows(i, carry):
        r = pl.ds(al(i * 16, 16), 16)
        err[r, :] = ((stu[r, :].astype(F32) - prj[r, :].astype(F32)) * factor).astype(BF)
        return carry

    lax.fori_loop(0, TOK // 16, err_rows, 0)

    LAST = NT - 2

    def others(fn):
        for o in range(NX):
            for w in range(NC):
                if o + w > 0:
                    fn(o * NC + w - 1, o, w)

    loads[3].wait()

    loads[5].wait()
    loads[6].wait()
    pre[...] = jnp.dot(Xs[t], wgu[pl.ds(al(t * S, S), S), :], preferred_element_type=F32)

    for o in range(1, NZ):
        arrived(RM.at[y, lax.rem(zh + NZ - o, NZ), x, c], rm_r.at[0, o - 1])
    for o in range(1, NY):
        send(RM.at[y, :, x, c], RM.at[y, :, x, c], rm_s.at[1], rm_r.at[1, o - 1], did(lax.rem(y + o, NY), zh, x, c, t))

    rest = pl.ds(1, NT - 1)
    for o in range(1, NT):
        arrived(WdS.at[o, wrow, ycols], wd_r.at[0, o - 1])
    for u in range(1, NY):
        send(
            WdS.at[rest, wrow, ycols], WdS.at[rest, wrow, ycols], wd_s.at[3, u - 1], wd_r.at[3, u - 1],
            did(lax.rem(y + u, NY), zh, x, c, t),
        )

    def tea_y(q, carry):
        q_y, q_c = lax.div(q, NC), lax.rem(q, NC)
        src = teacher.at[:, pl.ds(al((q_y * NC + q_c) * NP * ZT, NP * ZT), NP * ZT)]
        copy_or_send((q_y == y) & (q_c == c), src, TAy.at[yrow], ta_s, ta_r, did(q_y, zh, x, q_c, t))
        return carry

    lax.fori_loop(0, NY * NC, tea_y, 0)

    if LAST > 0:
        z_pass(0, 0)

    for o in range(1, NY):
        arrived(RM.at[lax.rem(y + NY - o, NY), :, x, c], rm_r.at[1, o - 1])
    others(lambda i, o, w: send(
        RM.at[:, :, x, c], RM.at[:, :, x, c], rm_s.at[2], rm_r.at[2, i], did(y, zh, lax.rem(x + o, NX), lax.rem(c + w, NC), t)
    ))

    for u in range(1, NY):
        cols = pl.ds(al(lax.rem(y + NY - u, NY) * SQ, SQ), SQ)
        arrived(WdS.at[rest, wrow, cols], wd_r.at[3, u - 1])
    for u in range(1, NX):
        send(WdS.at[rest, wrow], WdS.at[rest, wrow], wd_s.at[1, u - 1], wd_r.at[1, u - 1], did(y, zh, lax.rem(x + u, NX), c, t))

    a2a(t, 0, TOK)

    if LAST > 0:
        z_pass(0, 1)

    others(lambda i, o, w: arrived(RM.at[:, :, lax.rem(x + NX - o, NX), lax.rem(c + NC - w, NC)], rm_r.at[2, i]))

    @pl.when(t != 0)
    def _():
        arrived(eb, eb_r)

    ids = RM[...].reshape(DP, TOK)
    slot = jnp.sum(jnp.where((ids >> shift) == d, ids & (TOK - 1), 0), axis=1, keepdims=True)
    pick = (lax.broadcasted_iota(jnp.int32, (DP, TOK), 1) == slot).astype(F32).astype(BF)
    S0[...] = jnp.dot(pick, eb[...], preferred_element_type=F32).reshape(S0.shape)
    keep = [pltpu.make_async_copy(S0.at[:, :, x, c], S1.at[:, :, x, c], ea_l.at[0])]
    keep[0].start()

    def ea_out(i, o, w):
        q_x, q_c = lax.rem(x + o, NX), lax.rem(c + w, NC)
        send(S0.at[:, :, q_x, q_c], S1.at[:, :, x, c], ea_s.at[0], ea_r.at[0, i], did(y, zh, q_x, q_c, t))

    others(ea_out)

    if LAST > 0:
        z_each(0, a2a)
    if LAST > 1:
        z_pass(1, 0)

    keep[0].wait()
    others(lambda i, o, w: arrived(S1.at[:, :, lax.rem(x + NX - o, NX), lax.rem(c + NC - w, NC)], ea_r.at[0, i]))
    keep.append(pltpu.make_async_copy(S1.at[y], S2.at[y], ea_l.at[1]))
    keep[1].start()
    for o in range(1, NY):
        q = lax.rem(y + o, NY)
        send(S1.at[q], S2.at[y], ea_s.at[1], ea_r.at[1, o - 1], did(q, zh, x, c, t))

    if LAST > 1:
        z_pass(1, 1)

    if LAST > 1:
        z_each(1, a2a)

    keep[1].wait()
    for o in range(1, NY):
        arrived(S2.at[lax.rem(y + NY - o, NY)], ea_r.at[1, o - 1])
    for q in range(NZ):
        S3[q] = S2[:, q].reshape(DP // NZ, PB).astype(BF)
    for o in range(1, NZ):
        q = lax.rem(zh + o, NZ)
        send(S3.at[q], S4.at[zh], ea_s.at[2], ea_r.at[2, o - 1], did(y, q, x, c, t))
    S4[zh] = S3[zh]

    if LAST > 0:
        z_each(0, add_pre)
    for u in range(1, NX):
        r = pl.ds(al((c * NX + lax.rem(x + NX - u, NX)) * HR, HR), HR)
        arrived(WdS.at[rest, r], wd_r.at[1, u - 1])
    send(WdS.at[rest, crow], WdS.at[rest, crow], wd_s.at[2, 0], wd_r.at[2, 0], did(y, zh, x, 1 - c, t))

    loads[4].wait()
    arrived(WdS.at[rest, orow], wd_r.at[2, 0])
    for k in range(NT):
        actp[k] = lax.dot_general(err[...], WdS[k], (((1,), (1,)), ((), ())), preferred_element_type=F32)
    for k in range(1, NT):
        send(actp.at[k], actr.at[k - 1], act_s.at[k - 1], act_r.at[k - 1], (d, lax.rem(t + k, NT)))

    if LAST > 1:
        z_each(1, add_pre)

    hid, proj_rows = pl.ds(0, 2 * H), pl.ds(2 * H, PB)

    def along_y(rows, ssem, rsem):
        block = GEy.at[rows, yrow]
        for q_c in range(NC):
            for o in range(1, NY):
                send(block, block, ssem, rsem, did(lax.rem(y + o, NY), zh, x, q_c, t))
        send(block, block, ssem, rsem, did(y, zh, x, 1 - c, t))

    def along_x(ssem, rsem):
        block = GEx.at[:, xrow]
        for q_c in range(NC):
            for o in range(1, NX):
                send(block, block, ssem, rsem, did(y, zh, lax.rem(x + o, NX), q_c, t))
        send(block, block, ssem, rsem, did(y, zh, x, 1 - c, t))

    def z_last(h):
        z_pass(LAST, h)
        z_each(LAST, a2a, h * half, half)
        z_each(LAST, add_pre, h * half, half)

    z_last(0)

    for o in range(1, NZ):
        arrived(S4.at[lax.rem(zh + NZ - o, NZ)], ea_r.at[2, o - 1])
    row = lax.broadcasted_iota(jnp.int32, (DP, 1), 0)
    group, place = lax.div(row, DP // NZ), lax.rem(row, DP // NZ)
    row_d = (lax.div(place, NX * NC) * NZ + group) * (NX * NC) + lax.rem(place, NX * NC)
    order = ((RM[y, zh, x, c] >> shift) == row_d).astype(F32).astype(BF)
    GEy[proj_rows, yrow] = lax.dot_general(
        S4[...].reshape(DP, PB), order, (((0,), (0,)), ((), ())), preferred_element_type=F32
    ).astype(BF)

    along_y(proj_rows, e_s, e_r)

    for h in range(1, HALVES):
        z_last(h)

    act = actp[0]
    for o in range(1, NT):
        arrived(actr.at[o - 1], act_r.at[o - 1])
        act = act + actr[o - 1]
    gate_pre, up_pre = pre[:, 0:H], pre[:, H : 2 * H]
    sig = jax.nn.sigmoid(gate_pre)
    gate_grad = jnp.transpose(act * up_pre * sig * (1.0 + gate_pre * (1.0 - sig))).astype(BF)
    up_grad = jnp.transpose(act * gate_pre * sig).astype(BF)
    for buf, at in ((GEx, xrow), (GEy, yrow)):
        buf[0:H, at] = gate_grad
        buf[H : 2 * H, at] = up_grad
    along_x(g_s.at[1], g_r.at[1])
    along_y(hid, g_s.at[0], g_r.at[0])

    oy, ox = pl.ds(0, (NY * NC - 1) * TOK), pl.ds(0, (NX * NC - 1) * TOK)

    arrived(GEy.at[proj_rows, oy], e_r)
    arrived(TAy, ta_r)
    proj = jnp.transpose(jnp.dot(GEy[proj_rows, :], TAy[...], preferred_element_type=F32)).astype(BF)
    for q in range(NX):
        for j in range(NP):
            at = j * ZT + q * LT
            msgp[q, j * LT : (j + 1) * LT, :] = proj[at : at + LT, :]
        copy_or_send(q == x, msgp.at[q], RBX.at[x], rq_s.at[q], rq_r.at[x], did(y, zh, q, c, t))

    arrived(XAx, xa_r.at[1])
    arrived(GEx.at[:, ox], g_r.at[1])
    tot2 = jnp.dot(GEx[...], XAx[...], preferred_element_type=F32)
    for i in range(NS):
        for q_c in range(NC):
            at = (i * NC + q_c) * L
            msg2[i, q_c, :, 0:L] = tot2[:, at : at + L].astype(BF)
            s = c * NS + i
            copy_or_send(
                (s == y) & (q_c == c), msg2.at[i, q_c], RB2.at[y], r2_s.at[i, q_c], r2_r.at[y], did(s, zh, x, q_c, t)
            )
    arrived(XAy, xa_r.at[0])
    arrived(GEy.at[hid, oy], g_r.at[0])
    tot1 = jnp.dot(GEy[hid, :], XAy[...], preferred_element_type=F32)
    for q in range(NX):
        msg1[q, :, 0:L] = tot1[:, q * L : (q + 1) * L].astype(BF)
        copy_or_send(q == x, msg1.at[q], RB1.at[x], r1_s.at[q], r1_r.at[x], did(y, zh, q, c, t))

    part = None
    for q in range(NX):
        arrived(RBX.at[q], rq_r.at[q])
        part = RBX[q].astype(F32) if part is None else part + RBX[q].astype(F32)
    for j in range(NP):
        for q_c in range(NC):
            at = j * LT + q_c * RP
            finp[j, q_c] = part[at : at + RP, :].astype(BF)
            q_z = c * NP + j
            copy_or_send(
                (q_z == zh) & (q_c == c), finp.at[j, q_c], RBP.at[zh], rp_s.at[j, q_c], rp_r.at[zh], did(y, q_z, x, q_c, t)
            )
    for kind, (buf, sem, count, where) in enumerate(
        ((RB2, r2_r, NY, lambda q_c: (to_z, to_x, q_c)), (RB1, r1_r, NX, lambda q_c: (c, x, q_c)))
    ):
        part = None
        for q in range(count):
            arrived(buf.at[q], sem.at[q])
            part = buf[q].astype(F32) if part is None else part + buf[q].astype(F32)
        feats = jnp.transpose(part[:, 0:L])
        for q_c in range(NC):
            r = slice(q_c * R, (q_c + 1) * R)
            fin[kind, q_c, 0:R, :] = feats[r, 0:H].astype(BF)
            fin[kind, q_c, R : 2 * R, :] = feats[r, H : 2 * H].astype(BF)
            q_z, q_x, _ = where(q_c)
            copy_or_send(
                (q_z == zh) & (q_x == x) & (q_c == c), fin.at[kind, q_c], RB3.at[zh], rb_s.at[kind, q_c], rb_r.at[zh],
                did(y, q_z, q_x, q_c, t),
            )
    result = None
    for q in range(NZ):
        arrived(RB3.at[q], rb_r.at[q])
        result = RB3[q].astype(F32) if result is None else result + RB3[q].astype(F32)
    flipped = jnp.transpose(result)
    out[:, 0:R] = flipped[:, 0:R]
    out[:, R : 2 * R] = flipped[:, R : 2 * R]
    result = None
    for q in range(NZ):
        arrived(RBP.at[q], rp_r.at[q])
        result = RBP[q].astype(F32) if result is None else result + RBP[q].astype(F32)
    out[:, 2 * R : 2 * R + RP] = jnp.transpose(result)

    def left(own, ref, sem):
        @pl.when(jnp.logical_not(own))
        def _():
            arrived(ref, sem)

    for copy in drains:
        copy.wait_send()
    for k in range(NT - 1):
        for h in range(HALVES):
            z_drain(k, h)
    for o in range(1, NT):
        left(t != 0, eb, eb_s.at[o - 1])
    for q in range(NX):
        left(q == x, msg1.at[q], r1_s.at[q])
        left(q == x, msgp.at[q], rq_s.at[q])
    for q_c in range(NC):
        for i in range(NS):
            left((c * NS + i == y) & (q_c == c), msg2.at[i, q_c], r2_s.at[i, q_c])
        left((to_z == zh) & (to_x == x) & (q_c == c), fin.at[0, q_c], rb_s.at[0, q_c])
        left((c == zh) & (q_c == c), fin.at[1, q_c], rb_s.at[1, q_c])
        for j in range(NP):
            left((c * NP + j == zh) & (q_c == c), finp.at[j, q_c], rp_s.at[j, q_c])
    arrived(XAy.at[pl.ds(0, (NY * NC - 1) * TOK)], xa_s.at[0])
    arrived(XAx.at[pl.ds(0, (NX * NC - 1) * TOK)], xa_s.at[1])
    arrived(TAy.at[pl.ds(0, (NY * NC - 1) * TOK)], ta_s)


def solution(mesh, pb=128):
    dims = sizes(mesh, pb)
    NY, NX, NT = (dims[k] for k in ("NY", "NX", "NT"))

    def body(teacher_rows, row_map, student_hidden, projected, mlp_input, gate_bucket, up_bucket, down_bucket):
        TOK, S = mlp_input.shape
        F, H = gate_bucket.shape
        DTs = teacher_rows.shape[1]
        NS = NY // NC
        ZW, ZT = S // NZ, DTs // (NY * NZ)
        L, LT = ZW // NX, ZT // NX
        R, RP = L // NC, LT // NC
        NP = NZ // NC
        rows5 = (NY, NZ, NX, NC, 1)
        V, D = pltpu.VMEM, pltpu.SemaphoreType.DMA
        K = NT - 1
        scratch = [
            V((NT, TOK, S), BF), V((TOK, S), BF), V((TOK, S), BF), V((TOK, S), BF),
            V((F, 2 * H), BF), V((NT, H, S), BF),
            V((NY * NC * TOK, NP * ZT), BF),
            V((NY * NC * TOK, ZW), BF), V((NX * NC * TOK, NS * NC * L), BF),
            V((2 * H + pb, NY * NC * TOK), BF), V((2 * H, NX * NC * TOK), BF),
            V((TOK, 2 * H), F32), V((NT, TOK, H), F32), V((K, TOK, H), F32), V((TOK, pb), BF), V((2, TOK, pb), BF),
            V((*rows5, TOK), jnp.int32), *[V((*rows5, pb), F32)] * 3,
            *[V((NZ, NY * NX * NC, pb), BF)] * 2,
            V((NX, 2 * H, H), BF), V((NS, NC, 2 * H, H), BF), V((NX, NP * LT, pb), BF),
            V((NX, 2 * H, H), BF), V((NY, 2 * H, H), BF), V((NX, NP * LT, pb), BF),
            V((2, NC, 2 * R, H), BF), V((NP, NC, RP, H), BF), V((NZ, 2 * R, H), BF), V((NZ, RP, H), BF),
            D((9,)), D((2, K, HALVES)), D((2, K, HALVES)),
            D((4, 3)), D((4, 3)),
            D((K,)), D,
            D((3,)), D((3, NX * NC)), D((3,)), D((3, NX * NC)), D((3,)),
            D((2,)), D((2,)), D, D,
            D((K,)), D((K,)),
            D, D, D((2,)), D((2,)),
            D((NX,)), D((NX,)), D((NS, NC)), D((NY,)), D((NX,)), D((NX,)), D((2, NC)), D((NZ,)), D((NP, NC)), D((NZ,)),
        ]
        res = pl.pallas_call(
            functools.partial(kernel, dims),
            out_shape=jax.ShapeDtypeStruct((H, 2 * R + RP), F32),
            in_specs=[pl.BlockSpec(memory_space=pl.ANY)] * 8,
            out_specs=pl.BlockSpec(memory_space=pltpu.VMEM),
            scratch_shapes=scratch,
            compiler_params=pltpu.CompilerParams(
                collective_id=0, has_side_effects=True, vmem_limit_bytes=VMEM_LIMIT
            ),
        )(teacher_rows, row_map.reshape(1, TOK), student_hidden, projected, mlp_input, gate_bucket, up_bucket, down_bucket)
        return res[:, None, 2 * R :], res[:, :R], res[:, R : 2 * R]

    in_specs = (
        P("dp", "tensor"), P("dp"), P("dp", "tensor"), P("dp", "tensor"), P("dp", "tensor"),
        P(None, "tensor"), P(None, "tensor"), P("tensor", None),
    )
    out_specs = (P(None, "tensor", "dp"), P("tensor", "dp"), P("tensor", "dp"))
    return jax.shard_map(body, mesh=mesh, in_specs=in_specs, out_specs=out_specs, check_vma=False)
```
